32 devices in a mesh: pipe: 4 (over y, x), expert: 8 (over z, core).
Axes of the slice: x: 2, y: 2, z: 4, core: 2. Of those that a mesh axis runs over, the one named last changes fastest.
Arguments:
- stream_a: bfloat16 [4, 64, 3584], P('pipe', 'expert'), may hold values from -6 to 6
- stream_b: bfloat16 [4, 64, 3584], P('pipe', 'expert'), may hold values from -6 to 6
- routes: int32 [2, 2, 4, 64, 2], P(None, None, 'pipe', 'expert'), may hold values from 0 to 3, all different within a row; in each aligned block of 8 rows (0 to 7, 8 to 15, ..., all dimensions but the last counted through in order) at most 4 rows name the same one
- up_weight: bfloat16 [2, 4, 3584, 4096], P(None, 'pipe', None, 'expert'), as said below
- down_weight: bfloat16 [2, 4, 4096, 3584], P(None, 'pipe', 'expert'), as said below
- router_weight: bfloat16 [2, 4, 3584, 4], P(None, 'pipe'), as said below
Outputs:
- final_a: bfloat16 [4, 64, 3584], P('pipe', 'expert')
- final_b: bfloat16 [4, 64, 3584], P('pipe', 'expert')
- expert_load: float32 [4, 4], replicated
The draws below stay inside these ranges and needn't reach their ends.
Inputs may be any that keep to these rules, and one draw needn't show every extreme that they name: `routes`: in each device's 8 rows of one tick, stream and section, every expert is named by exactly 4 rows, and each row names 2 different experts. up_weight[1, i] equals up_weight[0, 3 - i]. down_weight[1, i] equals down_weight[0, 3 - i]. router_weight[1, i] equals router_weight[0, 3 - i].
All inputs are finite; a program needn't handle non-finite values.
Results may differ from the reference program's by a relative error of at most 0.0065.
Values may be sent and summed in bfloat16 or wider, within the bound.
No kernel may reach another device: no remote copies, remote signals or barrier semaphores. Data moves between devices by JAX's collectives and lax.ppermute only.
A program may use at most 64 MiB of HBM per device.

```python
import math
import jax
import jax.numpy as jnp
import numpy as np
from jax import lax

D = 3584
H_EXP = 1024
EXPERTS = 4
TOP = 2
ROWS = 8
TICKS = 2
LAYERS = 4
TOK_SECTION = 64
CAP = 4
N_EXPERT = 8


def mirrored(layer_draw):
    return jnp.stack([layer_draw, layer_draw[::-1]]).astype(jnp.bfloat16)


def draw_up_weight(key, part):
    key = jax.random.fold_in(key, 11)
    layer_draw = jax.random.normal(key, (LAYERS, D, EXPERTS * H_EXP), jnp.float32) * D ** (-0.5)
    return mirrored(layer_draw)


def draw_down_weight(key, part):
    key = jax.random.fold_in(key, 23)
    layer_draw = jax.random.normal(key, (LAYERS, EXPERTS * H_EXP, D), jnp.float32) * H_EXP ** (-0.5)
    return mirrored(layer_draw)


def draw_router_weight(key, part):
    key = jax.random.fold_in(key, 37)
    layer_draw = jax.random.normal(key, (LAYERS, D, EXPERTS), jnp.float32) * (2.0 * D ** (-0.5))
    return mirrored(layer_draw)


def shard_levels(rng, extent, cuts, smallest, largest):
    loudness, own = 1.0, jax.random.fold_in(rng, 6)
    for axis_at, parts in cuts:
        draws = jnp.exp(jax.random.uniform(jax.random.fold_in(own, axis_at), (parts,), jnp.float32, smallest / len(cuts), largest / len(cuts)))
        loudness = loudness * jnp.repeat(draws, extent[axis_at] // parts).reshape([-1 if axis == axis_at else 1 for axis in range(len(extent))])
    return loudness


def assign_block(key, own, number, rows, amount, top, reach, lean):
    ranking = jax.random.permutation(key, amount)
    heavy_load, ordinary = load_shares(amount, rows * top, reach, lean, True), load_shares(amount, rows * top, reach, lean, False)
    places = jnp.arange(amount)

    def named(sizes, rotation):
        used = int((sizes > 0).sum())
        fixed = max(1, used // 4)
        passed = fixed + (places - fixed + rotation * (used - fixed)) % max(1, amount - fixed)
        return jnp.zeros((amount,), jnp.int32).at[ranking[jnp.where(places < fixed, places, passed)]].set(jnp.asarray(sizes, jnp.int32))

    sizes = jnp.where(number % 4 == 0, named(heavy_load, number // 4), named(ordinary, number - number // 4 - 1))
    mixed = jax.random.permutation(jax.random.fold_in(own, 3), amount)
    giver, sink = mixed[0:amount // 2 * 2:2], mixed[1:amount // 2 * 2:2]
    room = jnp.minimum(sizes[giver] - 1, reach - sizes[sink]) // 2
    room = jnp.where((giver == ranking[0]) | (sink == ranking[0]) | (sizes[sink] == 0), 0, jnp.maximum(room, 0))
    passed = jax.random.randint(jax.random.fold_in(own, 4), (amount // 2,), 0, 1 << 20) % (room + 1)
    sizes = sizes.at[giver].add(-passed).at[sink].add(passed)
    labels = jnp.searchsorted(jnp.cumsum(sizes), jnp.arange(rows * top), side="right").astype(jnp.int32)
    table = labels.reshape(top, rows).T
    table = table[jax.random.permutation(jax.random.fold_in(own, 1), rows)]
    rotation = jax.random.randint(jax.random.fold_in(own, 2), (rows, 1), 0, top)
    return jnp.take_along_axis(table, (jnp.arange(top)[None, :] + rotation) % top, axis=1)


def load_shares(count, total, limit, skew, full):
    portions = [(1 << 20) // math.isqrt(grade ** skew) + 1 for grade in range(1, count + 1)]
    largest = limit if full else min(limit, max(-(-total // count), total * portions[0] // sum(portions)))
    least = 1 if total - largest >= count - 1 else 0
    holding, rest = [largest] + [least] * (count - 1), total - largest - least * (count - 1)
    while rest > 0:
        free = [i for i in range(1, count) if holding[i] < largest] or [i for i in range(1, count) if holding[i] < limit]
        whole, budget = sum([portions[i] for i in free]), rest
        for i in free:
            more = min(limit - holding[i], max(1, budget * portions[i] // whole), rest)
            holding[i] = holding[i] + more
            rest = rest - more
    return np.array(holding)


def bell_draw(stream_key, shape, width, reach, cuts=(), kind=jnp.bfloat16):
    array = width * jax.random.normal(stream_key, shape, jnp.float32)
    if cuts:
        array = array * shard_levels(stream_key, shape, cuts, -0.22, 0.18)
    return jnp.clip(array, -reach, reach).astype(kind)


def setup_inputs(seed: int = 0) -> dict:
    streams_of = jax.random.split(jax.random.key(seed), 7)
    stream_a = bell_draw(streams_of[0], (LAYERS, TOK_SECTION, D), 1.0, 6.0, ((0, 4), (1, 8)))
    stream_b = bell_draw(streams_of[1], (LAYERS, TOK_SECTION, D), 1.0, 6.0, ((0, 4), (1, 8)))
    routes_keys = jax.random.split(jax.random.fold_in(streams_of[2], 1), TICKS * 2 * LAYERS * TOK_SECTION // ROWS)
    routes_turns = jax.random.permutation(jax.random.fold_in(streams_of[2], 3), TICKS * 2 * LAYERS * TOK_SECTION // ROWS)
    routes = jax.vmap(lambda own, number: assign_block(jax.random.fold_in(streams_of[2], 2), own, number, ROWS, EXPERTS, TOP, CAP, 0))(routes_keys, routes_turns).reshape((TICKS, 2, LAYERS, TOK_SECTION, TOP))
    up_weight = draw_up_weight(jax.random.fold_in(streams_of[6], 71), 0)
    down_weight = draw_down_weight(jax.random.fold_in(streams_of[6], 71), 0)
    router_weight = draw_router_weight(jax.random.fold_in(streams_of[6], 71), 0)
    return dict(stream_a=stream_a, stream_b=stream_b, routes=routes, up_weight=up_weight, down_weight=down_weight, router_weight=router_weight)


EPS = 1e-06

def normalize(section_rows):
    widened = section_rows.astype(jnp.float32)
    return (widened * lax.rsqrt(lax.optimization_barrier(jnp.mean(widened * widened, axis=-1, keepdims=True)) + EPS)).astype(jnp.bfloat16)

def routing(normed, router, picked):
    experts = router.shape[-1]
    affinity = jax.nn.sigmoid(jnp.dot(normed, router, preferred_element_type=jnp.float32))
    member = (picked[:, :, None] == jnp.arange(experts, dtype=jnp.int32)[None, None, :]).astype(jnp.float32)
    chosen = lax.optimization_barrier(jnp.sum(member * affinity[:, None, :], axis=2))
    shares = chosen / lax.optimization_barrier(jnp.sum(chosen, axis=1, keepdims=True))
    weights = lax.optimization_barrier(jnp.sum(shares[:, :, None] * member, axis=1))
    selected = lax.optimization_barrier(jnp.sum(member, axis=1))
    return (weights, selected)

def apply_section(section_rows, lift_weight, lower_weight, router, picked):
    normed = normalize(section_rows)
    weights, selected = routing(normed, router, picked)
    experts = router.shape[-1]
    token_count = section_rows.shape[0]
    capacity = token_count * picked.shape[1] // experts
    group_size = N_EXPERT // experts
    hidden_width = lift_weight.shape[1] // experts
    slice_width = hidden_width // group_size
    features = section_rows.shape[1]
    total = jnp.zeros((token_count, features), jnp.float32)
    for expert in range(experts):
        flags = selected[:, expert].astype(jnp.int32)
        chosen_rows = jnp.argsort(1 - flags, stable=True)[:capacity].astype(jnp.int32)
        gathered = normed[chosen_rows]
        hidden = jax.nn.silu(jnp.dot(gathered, lift_weight[:, expert * hidden_width:(expert + 1) * hidden_width], preferred_element_type=jnp.float32)).astype(jnp.bfloat16)
        lower_part = lower_weight[expert * hidden_width:(expert + 1) * hidden_width].reshape(group_size, slice_width, features)
        pieces = jnp.einsum('rgk,gkd->grd', hidden.reshape(capacity, group_size, slice_width).astype(jnp.float32), lower_part.astype(jnp.float32), precision=lax.Precision.HIGHEST)
        rounded = lax.optimization_barrier(pieces.astype(jnp.bfloat16)).astype(jnp.float32)
        result = lax.optimization_barrier(jnp.sum(rounded, axis=0))
        total = total.at[chosen_rows].add(weights[chosen_rows, expert][:, None] * result)
    return ((section_rows.astype(jnp.float32) + total).astype(jnp.bfloat16), lax.optimization_barrier(jnp.sum(weights, axis=0)))

def apply_layer(bundle):
    return apply_section(bundle[0], bundle[1], bundle[2], bundle[3], bundle[4])

def reference(stream_a, stream_b, routes, up_weight, down_weight, router_weight):
    current = [stream_a, stream_b]
    load_sum = jnp.zeros((LAYERS, EXPERTS), jnp.float32)
    for step_index in range(TICKS):
        if step_index > 0:
            current = [jnp.roll(current[0], 1, axis=0), jnp.roll(current[1], -1, axis=0)]
        updated = []
        for stream in range(2):
            outcome, masses = lax.map(apply_layer, (current[stream], up_weight[stream], down_weight[stream], router_weight[stream], routes[step_index, stream]))
            updated.append(outcome)
            if stream == 0:
                load_sum = load_sum + masses
            else:
                load_sum = load_sum + masses[::-1]
        current = updated
    return (current[0], current[1], load_sum / (2 * TICKS * TOK_SECTION))
```

```python
import functools

import jax
import jax.numpy as jnp
from jax import lax
from jax.experimental import pallas as pl
from jax.experimental.pallas import tpu as pltpu
from jax.sharding import PartitionSpec as P

TICKS = 2


EPS = 1e-06

LANES = 128

STREAMS = 2

EARLY_FLOPS = 2 * 10**10

TABLE_ROWS = 64


def in_hbm(array):
    return pltpu.with_memory_space_constraint(array, pltpu.HBM)


def in_vmem(array):
    return pltpu.with_memory_space_constraint(array, pltpu.VMEM)


def call(
    body, outs, name, flops=0, size=0, in_specs=None, out_specs=None, scratch=(), inputs=0, held=()
):
    more = {}
    if held:
        in_specs = [pl.BlockSpec(memory_space=pltpu.VMEM)] * (inputs + len(held))

        def whole_body(*refs):
            body(*refs[:inputs], *refs[inputs + len(held) :])

        result = call(whole_body, outs, name, flops, size, in_specs, out_specs, scratch)
        return lambda *operands: result(*operands, *[in_vmem(value) for value in held])
    if in_specs is not None:
        more["in_specs"] = in_specs
    if out_specs is not None:
        more["out_specs"] = out_specs
    return pl.pallas_call(
        body,
        out_shape=outs,
        name=name,
        scratch_shapes=scratch,
        cost_estimate=pl.CostEstimate(flops=flops, bytes_accessed=size, transcendentals=0),
        compiler_params=pltpu.CompilerParams(vmem_limit_bytes=8 << 20),
        **more,
    )


def lane_ids(rows, width=LANES):
    return lax.broadcasted_iota(jnp.int32, (rows, width), 1)


def is_even(place, shape):
    return (lax.broadcasted_iota(jnp.int32, shape, 0) * 0 + place) % 2 == 0


def upright(row):
    n = row.shape[1]
    square = jnp.broadcast_to(row, (n, n))
    diagonal = lax.broadcasted_iota(jnp.int32, (n, n), 0) == lax.broadcasted_iota(
        jnp.int32, (n, n), 1
    )
    return jnp.sum(jnp.where(diagonal, square, 0.0), axis=1, keepdims=True)


def normalize(x):
    wide = x.astype(jnp.float32)
    return (wide * lax.rsqrt(jnp.mean(wide * wide, axis=-1, keepdims=True) + EPS)).astype(
        jnp.bfloat16
    )


def chosen_by(picks):
    return [upright(picks[i : i + 1, :].astype(jnp.float32)).astype(jnp.int32) for i in range(2)]


def place_rows(chosen, mine, rows, capacity):
    lanes = lane_ids(rows)
    rows_at = lax.broadcasted_iota(jnp.int32, (rows, LANES), 0)
    kind = lanes // capacity
    named = ((chosen[0] ^ mine) == kind) | ((chosen[1] ^ mine) == kind)
    named_f = jnp.where(named, 1.0, 0.0)
    before = jnp.zeros((rows, LANES), jnp.float32)
    for r in range(rows - 1):
        before = before + jnp.where(rows_at > r, named_f[r : r + 1, :], 0.0)
    slot = named & (before == (lanes % capacity).astype(jnp.float32))
    return jnp.where(slot, 1.0, 0.0)


def pack_rows(place, normed, slots):
    return jnp.dot(
        place.T[:slots].astype(jnp.bfloat16), normed, preferred_element_type=jnp.float32
    )


def gate_rows(normed, router, chosen, place, me, mine, experts, capacity, spare):
    rows = normed.shape[0]
    wide = normed.astype(jnp.float32)
    taken = [jnp.zeros((rows, 1), jnp.float32) for _ in range(2)]
    for e in range(experts):
        affinity = jax.nn.sigmoid(
            jnp.sum(wide * router[e : e + 1, :].astype(jnp.float32), axis=1, keepdims=True)
        )
        taken = [jnp.where(pick == e, affinity, old) for pick, old in zip(chosen, taken)]
    whole = taken[0] + taken[1]
    shares = [taken[0] / whole, taken[1] / whole]
    kind = lane_ids(rows) // capacity
    share_at = jnp.where((chosen[0] ^ mine) == kind, shares[0], 0.0) + jnp.where(
        (chosen[1] ^ mine) == kind, shares[1], 0.0
    )
    spread = lane_ids(rows, spare)
    masses = []
    for shift in (0, experts):
        base = me * 2 * experts + shift
        here = jnp.where(spread == chosen[0] + base, shares[0], 0.0)
        here = here + jnp.where(spread == chosen[1] + base, shares[1], 0.0)
        masses.append(jnp.sum(here, axis=0, keepdims=True))
    return place * share_at, jnp.concatenate(masses)


def carry_masses(masses):
    top = masses.astype(jnp.bfloat16).astype(jnp.float32)
    return top[:1] + (masses - top)[1:]


def store_blocks(packed, block_refs, capacity):
    features = packed[0].shape[1]
    for k, block_ref in enumerate(block_refs):
        rows = [part[k * capacity : (k + 1) * capacity] for part in packed]
        block_ref[:, :features] = jnp.concatenate(rows).astype(jnp.bfloat16)


def prepare_body(group, experts, capacity, *refs):
    sources, me_ref = refs[:4], refs[4]
    block_refs = refs[5 : 5 + experts]
    x_ref, normed_ref, place_ref, router_ref, routes_ref, sems = refs[5 + experts :]
    targets = [x_ref.at[0], x_ref.at[1], router_ref, routes_ref]
    copies = [
        pltpu.make_async_copy(source, target, sems.at[i])
        for i, (source, target) in enumerate(zip(sources, targets))
    ]
    for copy in copies:
        copy.start()
    mine = lax.div(me_ref[0, 0], group)
    rows = x_ref.shape[1]
    copies[3].wait()
    places = [
        place_rows(chosen_by(routes_ref[0, stream]), mine, rows, capacity)
        for stream in range(STREAMS)
    ]
    for copy in copies[:3]:
        copy.wait()
    packed = []
    for stream in range(STREAMS):
        normed = normalize(x_ref[stream])
        normed_ref[stream] = normed
        place_ref[stream] = places[stream]
        packed.append(pack_rows(places[stream], normed, experts * capacity))
    store_blocks(packed, block_refs, capacity)


def prepare(inputs, group, capacity):
    x, _, router, routes, _ = inputs
    rows, features = x.shape
    experts = router.shape[1]
    both = jax.ShapeDtypeStruct((STREAMS, rows, features), jnp.bfloat16)
    outs = [
        jax.ShapeDtypeStruct((STREAMS * capacity, features), jnp.bfloat16) for _ in range(experts)
    ]
    outs += [
        both,
        both,
        jax.ShapeDtypeStruct((STREAMS, rows, LANES), jnp.float32),
        jax.ShapeDtypeStruct(router.shape, router.dtype),
        jax.ShapeDtypeStruct(routes.shape, routes.dtype),
    ]
    result = call(
        functools.partial(prepare_body, group, experts, capacity),
        outs,
        "prepare",
        EARLY_FLOPS,
        4 * rows * features,
        [pl.BlockSpec(memory_space=pl.ANY)] * 4 + [pl.BlockSpec(memory_space=pltpu.VMEM)],
        None,
        [pltpu.SemaphoreType.DMA((4,))],
    )(*[in_hbm(value) for value in inputs[:4]], inputs[4])
    return result[:experts], result[experts:]


def gates_body(group, experts, capacity, spare, *refs):
    normed_ref, place_ref, router_ref, routes_ref, me_ref = refs[:5]
    coefficient_ref, mass_ref, next_ref = refs[5:]
    me = me_ref[0, 0]
    mine = lax.div(me, group)
    rows = normed_ref.shape[1]
    for stream in range(STREAMS):
        coefficient_ref[stream], mass_ref[stream] = gate_rows(
            normed_ref[stream],
            router_ref[stream],
            chosen_by(routes_ref[0, stream]),
            place_ref[stream],
            me,
            mine,
            experts,
            capacity,
            spare,
        )
        next_ref[stream] = place_rows(chosen_by(routes_ref[1, stream]), mine, rows, capacity)


def gates(normed, place, router, routes, me, group, capacity, spare):
    experts = router.shape[1]
    outs = [
        jax.ShapeDtypeStruct(place.shape, jnp.float32),
        jax.ShapeDtypeStruct((STREAMS, 2, spare), jnp.float32),
        jax.ShapeDtypeStruct(place.shape, jnp.float32),
    ]
    return call(
        functools.partial(gates_body, group, experts, capacity, spare),
        outs,
        "gates",
        32 * normed.size,
        4 * normed.size,
    )(normed, place, router, routes, me)


def repeat_body(group, experts, capacity, spare, *refs):
    far_ref, near_ref, place_ref, router_ref, routes_ref, old_ref, me_ref = refs[:7]
    block_refs = refs[7 : 7 + experts]
    x_ref, coefficient_ref = refs[7 + experts :]
    me = me_ref[0, 0]
    mine = lax.div(me, group)
    far, near = far_ref[...], near_ref[...]
    features = near.shape[1]
    even = is_even(me_ref[0, 1], near.shape)
    xs = [jnp.where(even, far, near), jnp.where(even, near, far)]
    packed, carried = [], []
    for stream in range(STREAMS):
        x_ref[stream] = xs[stream]
        normed = normalize(xs[stream])
        packed.append(pack_rows(place_ref[stream], normed, experts * capacity))
        coefficient, masses = gate_rows(
            normed,
            router_ref[stream],
            chosen_by(routes_ref[1, stream]),
            place_ref[stream],
            me,
            mine,
            experts,
            capacity,
            spare,
        )
        coefficient_ref[stream] = coefficient
        carried.append(
            jnp.broadcast_to(carry_masses(masses + old_ref[stream]), (capacity, spare))
        )
    store_blocks(packed, block_refs, capacity)
    carried = jnp.concatenate(carried).astype(jnp.bfloat16)
    for block_ref in block_refs:
        block_ref[:, features:] = carried


def repeat(inputs, group, capacity, spare, held):
    near, place, router = inputs[1:4]
    rows, features = near.shape
    experts = router.shape[1]
    outs = [
        jax.ShapeDtypeStruct((STREAMS * capacity, features + spare), jnp.bfloat16)
        for _ in range(experts)
    ]
    outs += [
        jax.ShapeDtypeStruct((STREAMS, rows, features), jnp.bfloat16),
        jax.ShapeDtypeStruct(place.shape, jnp.float32),
    ]
    result = call(
        functools.partial(repeat_body, group, experts, capacity, spare),
        outs,
        "prepare",
        512 * rows * features,
        4 * rows * features,
        inputs=len(inputs),
        held=held,
    )(*inputs)
    return result[:experts], result[experts:]


def order_of(experts):
    return [0, *range(experts - 1, 0, -1)]


def shuffled(parts):
    return [parts[k] for k in order_of(len(parts))]


def arranged(parts):
    order = order_of(len(parts))
    return [parts[order.index(k)] for k in range(len(parts))]


def join_body(capacity, experts, *refs):
    parts, out_ref = arranged(refs[:experts]), refs[-1]
    rows = [part[...].astype(jnp.float32) for part in parts]
    out_ref[...] = jnp.concatenate(
        [
            part[stream * capacity : (stream + 1) * capacity]
            for stream in range(STREAMS)
            for part in rows
        ]
    ).astype(out_ref.dtype)


def join(parts, capacity, after=()):
    shape = (sum(part.shape[0] for part in parts), parts[0].shape[1])
    return call(
        functools.partial(join_body, capacity, len(parts)),
        jax.ShapeDtypeStruct(shape, parts[0].dtype),
        "join",
        0,
        4 * shape[0] * shape[1],
        [pl.BlockSpec(memory_space=pltpu.VMEM)] * (len(parts) + len(after)),
    )(*shuffled(parts), *after)


def expert_body(group, capacity, experts, spare, layers, up_ref, down_ref, *refs):
    refs = list(refs)
    if spare:
        place_ref = refs.pop(0)
    batch_refs = refs[:group]
    out_refs = refs[group : 2 * group]
    features, hidden_width = up_ref.shape[1:]
    block = batch_refs[0].shape[0] // STREAMS
    for stream in range(STREAMS):
        mine = slice(stream * block, (stream + 1) * block)
        rows = jnp.concatenate([ref[mine, :features] for ref in batch_refs])
        raw = jnp.dot(rows, up_ref[stream], preferred_element_type=jnp.float32)
        hidden = jax.nn.silu(raw).astype(jnp.bfloat16)
        value = jnp.dot(hidden, down_ref[stream], preferred_element_type=jnp.float32)
        for h in range(group):
            out_refs[h][mine, :] = value[h * block : (h + 1) * block].astype(jnp.bfloat16)
    if spare:
        table_ref = refs[2 * group]
        place = place_ref[0, 1]
        rows = table_ref.shape[0]
        at = lane_ids(1, spare) % experts
        lanes = lane_ids(rows)
        ladder = lax.broadcasted_iota(jnp.int32, (rows, LANES), 0)
        table = jnp.zeros((rows, LANES), jnp.float32)
        for stream in range(STREAMS):
            total = jnp.zeros((1, spare), jnp.float32)
            for ref in batch_refs:
                values = ref[:, features:].astype(jnp.float32)
                for k in range(experts):
                    row = stream * block + k * capacity
                    total = total + values[row : row + 1]
            row = place if stream == 0 else layers - 1 - place
            for e in range(experts):
                value = jnp.sum(jnp.where(at == e, total, 0.0), axis=1, keepdims=True)
                table = table + jnp.where((ladder == row) & (lanes == e), value, 0.0)
        table_ref[...] = table


def expert_rows(batch, up, down, capacity, experts, spare, place=None, layers=0):
    group = len(batch)
    features, hidden_width = up.shape[1:]
    rows = batch[0].shape[0]
    outs = [jax.ShapeDtypeStruct((rows, features), jnp.bfloat16) for _ in range(group)]
    inputs = [in_vmem(up), in_vmem(down)]
    if spare:
        outs.append(jax.ShapeDtypeStruct((-(-layers // TABLE_ROWS) * TABLE_ROWS, LANES), jnp.float32))
        inputs.append(place)
    inputs += batch
    in_place = pl.BlockSpec(memory_space=pltpu.VMEM)
    return call(
        functools.partial(expert_body, group, capacity, experts, spare, layers),
        outs,
        "experts",
        4 * group * rows * features * hidden_width,
        2 * up.size,
        [in_place] * len(inputs),
    )(*inputs)


def add_body(experts, capacity, *refs):
    parts = refs[:-experts]
    summed = sum(part[...].astype(jnp.float32) for part in parts)
    block = summed.shape[0] // STREAMS
    for k in range(experts):
        refs[len(parts) + k][...] = jnp.concatenate(
            [
                summed[stream * block + k * capacity : stream * block + (k + 1) * capacity]
                for stream in range(STREAMS)
            ]
        ).astype(jnp.bfloat16)


def add_up(parts, experts, capacity, held=()):
    rows, features = parts[0].shape
    outs = [
        jax.ShapeDtypeStruct((rows // experts, features), jnp.bfloat16) for _ in range(experts)
    ]
    return call(
        functools.partial(add_body, experts, capacity),
        outs,
        "add_up",
        0,
        4 * rows * features,
        inputs=len(parts),
        held=held,
    )(*parts)


def finish_body(experts, capacity, scale, x_ref, me_ref, coefficient_ref, *refs):
    parts = [ref[...].astype(jnp.float32) for ref in arranged(refs[:experts])]
    rest = refs[experts:]
    results = []
    for stream in range(STREAMS):
        returned = jnp.concatenate(
            [part[stream * capacity : (stream + 1) * capacity] for part in parts]
        ).astype(jnp.bfloat16)
        coefficient = coefficient_ref[stream, :, : experts * capacity]
        high = coefficient.astype(jnp.bfloat16)
        low = (coefficient - high.astype(jnp.float32)).astype(jnp.bfloat16)
        mixture = jnp.dot(high, returned, preferred_element_type=jnp.float32) + jnp.dot(
            low, returned, preferred_element_type=jnp.float32
        )
        results.append(x_ref[stream].astype(jnp.float32) + mixture)
    if not scale:
        even = is_even(me_ref[0, 1], mixture.shape)
        results = [
            jnp.where(even, results[1], results[0]),
            jnp.where(even, results[0], results[1]),
        ]
    for out_ref, result in zip(rest[-STREAMS - 1 :] if scale else rest, results):
        out_ref[...] = result.astype(out_ref.dtype)
    if scale:
        layers = rest[-1].shape[0]
        table = sum(ref[:layers, :] for ref in rest[: -STREAMS - 1])
        rest[-1][...] = table[:, :experts] / scale


def finish(x, me, coefficient, parts, capacity, layers, tables=(), scale=0.0, held=()):
    experts = len(parts)
    rows, features = coefficient.shape[1], parts[0].shape[1]
    outs = [jax.ShapeDtypeStruct((rows, features), jnp.bfloat16) for _ in range(STREAMS)]
    if scale:
        outs.append(jax.ShapeDtypeStruct((layers, experts), jnp.float32))
    return call(
        functools.partial(finish_body, experts, capacity, scale),
        outs,
        "finish",
        128 * rows * features,
        12 * rows * features,
        inputs=3 + experts + len(tables),
        held=held,
    )(x, me, coefficient, *shuffled(parts), *tables)


class Ring:
    def __init__(self, experts):
        self.pipe = lax.axis_size("pipe")
        self.size = lax.axis_size("expert")
        self.experts = experts
        self.group = self.size // experts

    def across(self, blocks):
        moved = {0: blocks[0]}
        for k in sorted(range(1, self.experts), key=lambda k: -k):
            moved[k] = lax.ppermute(
                blocks[k], "expert", [(j, j ^ (k * self.group)) for j in range(self.size)]
            )
        return [moved[k] for k in range(self.experts)]

    def within(self, array, shift):
        pairs = [
            (j, j // self.group * self.group + (j + shift) % self.group) for j in range(self.size)
        ]
        return lax.ppermute(array, "expert", pairs)

    def far(self, array):
        steps = [(i + 1 if i % 2 else i - 1) % self.pipe for i in range(self.pipe)]
        return lax.ppermute(array, "pipe", list(enumerate(steps)))

    def near(self, array):
        return lax.ppermute(array, "pipe", [(i, i ^ 1) for i in range(self.pipe)])

    def over_sections(self, table):
        if self.pipe & (self.pipe - 1):
            return [lax.psum(table, "pipe")]
        parts = [table]
        step = 1
        while step < self.pipe:
            table = sum(parts[1:], parts[0])[: table.shape[0] if step == 1 else self.pipe]
            moved = lax.ppermute(table, "pipe", [(i, i ^ step) for i in range(self.pipe)])
            parts = [table, moved]
            step *= 2
        return parts


def shards(stream_a, stream_b, routes, up_weight, down_weight, router_weight):
    experts = router_weight.shape[-1]
    ring = Ring(experts)
    rows, features = stream_a.shape[1:]
    capacity = rows * routes.shape[-1] // experts
    me = jnp.stack([lax.axis_index("expert"), lax.axis_index("pipe")]).astype(jnp.int32)[None]
    router = jnp.swapaxes(router_weight[:, 0], 1, 2)
    picks = jnp.swapaxes(routes[:, :, 0], 2, 3)
    spare = -(-2 * experts * ring.size // LANES) * LANES
    tokens_total = 2 * TICKS * rows * ring.size
    up, down = up_weight[:, 0], down_weight[:, 0]
    held = ()
    for step in range(TICKS):
        first, last = step == 0, step == TICKS - 1
        room = spare if last else 0
        if first:
            blocks, others = prepare(
                [stream_a[0], stream_b[0], router, picks, me], ring.group, capacity
            )
            x, normed, slots, router, picks = others
            coefficient, mass, slots = gates(
                normed, slots, router, picks, me, ring.group, capacity, spare
            )
        else:
            blocks, (x, coefficient) = repeat(
                [*moved, slots, router, picks, mass, me], ring.group, capacity, spare, held
            )
        own = join(
            ring.across(blocks),
            capacity,
            [in_vmem(value) for value in held],
        )
        batch = [own] + [ring.within(own, h) for h in range(1, ring.group)]
        values = expert_rows(batch, up, down, capacity, experts, room, me, ring.pipe)
        held = () if last else (up, down)
        back = add_up(
            [values[0]] + [ring.within(values[h], -h) for h in range(1, ring.group)],
            experts,
            capacity,
            held,
        )
        tables = ring.over_sections(values[-1]) if last else ()
        result = finish(
            x,
            me,
            coefficient,
            ring.across(back),
            capacity,
            ring.pipe,
            tables,
            float(tokens_total) if last else 0.0,
            held,
        )
        if not last:
            moved = [ring.far(result[0]), ring.near(result[1])]
    return (result[0][None], result[1][None], result[2])


def solution(mesh):
    return jax.shard_map(
        shards,
        mesh=mesh,
        in_specs=(
            P("pipe", "expert", None),
            P("pipe", "expert", None),
            P(None, None, "pipe", "expert", None),
            P(None, "pipe", None, "expert"),
            P(None, "pipe", "expert", None),
            P(None, "pipe", None, None),
        ),
        out_specs=(P("pipe", "expert", None), P("pipe", "expert", None), P()),
        check_vma=False,
    )
```

```python
import functools

import jax
import jax.numpy as jnp
from jax import lax
from jax.experimental import pallas as pl
from jax.experimental.pallas import tpu as pltpu
from jax.sharding import PartitionSpec as P

TICKS = 2


EPS = 1e-06

LANES = 128

STREAMS = 2

EARLY_FLOPS = 2 * 10**10

TABLE_ROWS = 64


def in_hbm(array):
    return pltpu.with_memory_space_constraint(array, pltpu.HBM)


def in_vmem(array):
    return pltpu.with_memory_space_constraint(array, pltpu.VMEM)


def call(
    body, outs, name, flops=0, size=0, in_specs=None, out_specs=None, scratch=(), inputs=0, held=()
):
    more = {}
    if held:
        in_specs = [pl.BlockSpec(memory_space=pltpu.VMEM)] * (inputs + len(held))

        def whole_body(*refs):
            body(*refs[:inputs], *refs[inputs + len(held) :])

        result = call(whole_body, outs, name, flops, size, in_specs, out_specs, scratch)
        return lambda *operands: result(*operands, *[in_vmem(value) for value in held])
    if in_specs is not None:
        more["in_specs"] = in_specs
    if out_specs is not None:
        more["out_specs"] = out_specs
    return pl.pallas_call(
        body,
        out_shape=outs,
        name=name,
        scratch_shapes=scratch,
        cost_estimate=pl.CostEstimate(flops=flops, bytes_accessed=size, transcendentals=0),
        compiler_params=pltpu.CompilerParams(vmem_limit_bytes=8 << 20),
        **more,
    )


def lane_ids(rows, width=LANES):
    return lax.broadcasted_iota(jnp.int32, (rows, width), 1)


def is_even(place, shape):
    return (lax.broadcasted_iota(jnp.int32, shape, 0) * 0 + place) % 2 == 0


def upright(row):
    n = row.shape[1]
    square = jnp.broadcast_to(row, (n, n))
    diagonal = lax.broadcasted_iota(jnp.int32, (n, n), 0) == lax.broadcasted_iota(
        jnp.int32, (n, n), 1
    )
    return jnp.sum(jnp.where(diagonal, square, 0.0), axis=1, keepdims=True)


def normalize(x):
    wide = x.astype(jnp.float32)
    return (wide * lax.rsqrt(jnp.mean(wide * wide, axis=-1, keepdims=True) + EPS)).astype(
        jnp.bfloat16
    )


def chosen_by(picks):
    return [upright(picks[i : i + 1, :].astype(jnp.float32)).astype(jnp.int32) for i in range(2)]


def place_rows(chosen, mine, rows, capacity):
    lanes = lane_ids(rows)
    rows_at = lax.broadcasted_iota(jnp.int32, (rows, LANES), 0)
    kind = lanes // capacity
    named = ((chosen[0] ^ mine) == kind) | ((chosen[1] ^ mine) == kind)
    named_f = jnp.where(named, 1.0, 0.0)
    before = jnp.zeros((rows, LANES), jnp.float32)
    for r in range(rows - 1):
        before = before + jnp.where(rows_at > r, named_f[r : r + 1, :], 0.0)
    slot = named & (before == (lanes % capacity).astype(jnp.float32))
    return jnp.where(slot, 1.0, 0.0)


def pack_rows(place, normed, slots):
    return jnp.dot(
        place.T[:slots].astype(jnp.bfloat16), normed, preferred_element_type=jnp.float32
    )


def gate_rows(normed, router, chosen, place, me, mine, experts, capacity, spare):
    rows = normed.shape[0]
    wide = normed.astype(jnp.float32)
    taken = [jnp.zeros((rows, 1), jnp.float32) for _ in range(2)]
    for e in range(experts):
        affinity = jax.nn.sigmoid(
            jnp.sum(wide * router[e : e + 1, :].astype(jnp.float32), axis=1, keepdims=True)
        )
        taken = [jnp.where(pick == e, affinity, old) for pick, old in zip(chosen, taken)]
    whole = taken[0] + taken[1]
    shares = [taken[0] / whole, taken[1] / whole]
    kind = lane_ids(rows) // capacity
    share_at = jnp.where((chosen[0] ^ mine) == kind, shares[0], 0.0) + jnp.where(
        (chosen[1] ^ mine) == kind, shares[1], 0.0
    )
    spread = lane_ids(rows, spare)
    masses = []
    for shift in (0, experts):
        base = me * 2 * experts + shift
        here = jnp.where(spread == chosen[0] + base, shares[0], 0.0)
        here = here + jnp.where(spread == chosen[1] + base, shares[1], 0.0)
        masses.append(jnp.sum(here, axis=0, keepdims=True))
    return place * share_at, jnp.concatenate(masses)


def carry_masses(masses):
    top = masses.astype(jnp.bfloat16).astype(jnp.float32)
    return top[:1] + (masses - top)[1:]


def store_blocks(packed, block_refs, capacity):
    features = packed[0].shape[1]
    for k, block_ref in enumerate(block_refs):
        rows = [part[k * capacity : (k + 1) * capacity] for part in packed]
        block_ref[:, :features] = jnp.concatenate(rows).astype(jnp.bfloat16)


def prepare_body(group, experts, capacity, *refs):
    sources, me_ref = refs[:4], refs[4]
    block_refs = refs[5 : 5 + experts]
    x_ref, normed_ref, place_ref, router_ref, routes_ref, sems = refs[5 + experts :]
    targets = [x_ref.at[0], x_ref.at[1], router_ref, routes_ref]
    copies = [
        pltpu.make_async_copy(source, target, sems.at[i])
        for i, (source, target) in enumerate(zip(sources, targets))
    ]
    for copy in copies:
        copy.start()
    mine = lax.div(me_ref[0, 0], group)
    rows = x_ref.shape[1]
    copies[3].wait()
    places = [
        place_rows(chosen_by(routes_ref[0, stream]), mine, rows, capacity)
        for stream in range(STREAMS)
    ]
    for copy in copies[:3]:
        copy.wait()
    packed = []
    for stream in range(STREAMS):
        normed = normalize(x_ref[stream])
        normed_ref[stream] = normed
        place_ref[stream] = places[stream]
        packed.append(pack_rows(places[stream], normed, experts * capacity))
    store_blocks(packed, block_refs, capacity)


def prepare(inputs, group, capacity):
    x, _, router, routes, _ = inputs
    rows, features = x.shape
    experts = router.shape[1]
    both = jax.ShapeDtypeStruct((STREAMS, rows, features), jnp.bfloat16)
    outs = [
        jax.ShapeDtypeStruct((STREAMS * capacity, features), jnp.bfloat16) for _ in range(experts)
    ]
    outs += [
        both,
        both,
        jax.ShapeDtypeStruct((STREAMS, rows, LANES), jnp.float32),
        jax.ShapeDtypeStruct(router.shape, router.dtype),
        jax.ShapeDtypeStruct(routes.shape, routes.dtype),
    ]
    result = call(
        functools.partial(prepare_body, group, experts, capacity),
        outs,
        "prepare",
        EARLY_FLOPS,
        4 * rows * features,
        [pl.BlockSpec(memory_space=pl.ANY)] * 4 + [pl.BlockSpec(memory_space=pltpu.VMEM)],
        None,
        [pltpu.SemaphoreType.DMA((4,))],
    )(*[in_hbm(value) for value in inputs[:4]], inputs[4])
    return result[:experts], result[experts:]


def gates_body(group, experts, capacity, spare, *refs):
    normed_ref, place_ref, router_ref, routes_ref, me_ref = refs[:5]
    coefficient_ref, mass_ref, next_ref = refs[5:]
    me = me_ref[0, 0]
    mine = lax.div(me, group)
    rows = normed_ref.shape[1]
    for stream in range(STREAMS):
        coefficient_ref[stream], mass_ref[stream] = gate_rows(
            normed_ref[stream],
            router_ref[stream],
            chosen_by(routes_ref[0, stream]),
            place_ref[stream],
            me,
            mine,
            experts,
            capacity,
            spare,
        )
        next_ref[stream] = place_rows(chosen_by(routes_ref[1, stream]), mine, rows, capacity)


def gates(normed, place, router, routes, me, group, capacity, spare):
    experts = router.shape[1]
    outs = [
        jax.ShapeDtypeStruct(place.shape, jnp.float32),
        jax.ShapeDtypeStruct((STREAMS, 2, spare), jnp.float32),
        jax.ShapeDtypeStruct(place.shape, jnp.float32),
    ]
    return call(
        functools.partial(gates_body, group, experts, capacity, spare),
        outs,
        "gates",
        32 * normed.size,
        4 * normed.size,
    )(normed, place, router, routes, me)


def repeat_body(group, experts, capacity, spare, *refs):
    far_ref, near_ref, place_ref, router_ref, routes_ref, old_ref, me_ref = refs[:7]
    block_refs = refs[7 : 7 + experts]
    x_ref, coefficient_ref = refs[7 + experts :]
    me = me_ref[0, 0]
    mine = lax.div(me, group)
    far, near = far_ref[...], near_ref[...]
    features = near.shape[1]
    even = is_even(me_ref[0, 1], near.shape)
    xs = [jnp.where(even, far, near), jnp.where(even, near, far)]
    packed, carried = [], []
    for stream in range(STREAMS):
        x_ref[stream] = xs[stream]
        normed = normalize(xs[stream])
        packed.append(pack_rows(place_ref[stream], normed, experts * capacity))
        coefficient, masses = gate_rows(
            normed,
            router_ref[stream],
            chosen_by(routes_ref[1, stream]),
            place_ref[stream],
            me,
            mine,
            experts,
            capacity,
            spare,
        )
        coefficient_ref[stream] = coefficient
        carried.append(
            jnp.broadcast_to(carry_masses(masses + old_ref[stream]), (capacity, spare))
        )
    store_blocks(packed, block_refs, capacity)
    carried = jnp.concatenate(carried).astype(jnp.bfloat16)
    for block_ref in block_refs:
        block_ref[:, features:] = carried


def repeat(inputs, group, capacity, spare, held):
    near, place, router = inputs[1:4]
    rows, features = near.shape
    experts = router.shape[1]
    outs = [
        jax.ShapeDtypeStruct((STREAMS * capacity, features + spare), jnp.bfloat16)
        for _ in range(experts)
    ]
    outs += [
        jax.ShapeDtypeStruct((STREAMS, rows, features), jnp.bfloat16),
        jax.ShapeDtypeStruct(place.shape, jnp.float32),
    ]
    result = call(
        functools.partial(repeat_body, group, experts, capacity, spare),
        outs,
        "prepare",
        512 * rows * features,
        4 * rows * features,
        inputs=len(inputs),
        held=held,
    )(*inputs)
    return result[:experts], result[experts:]


def order_of(experts, out):
    return [0, *range(2, experts), 1] if out else [0, *range(experts - 1, 0, -1)]


def shuffled(parts, out):
    return [parts[k] for k in order_of(len(parts), out)]


def arranged(parts, out):
    order = order_of(len(parts), out)
    return [parts[order.index(k)] for k in range(len(parts))]


def join_body(capacity, experts, *refs):
    parts, out_ref = arranged(refs[:experts], True), refs[-1]
    rows = [part[...].astype(jnp.float32) for part in parts]
    out_ref[...] = jnp.concatenate(
        [
            part[stream * capacity : (stream + 1) * capacity]
            for stream in range(STREAMS)
            for part in rows
        ]
    ).astype(out_ref.dtype)


def join(parts, capacity, after=()):
    shape = (sum(part.shape[0] for part in parts), parts[0].shape[1])
    return call(
        functools.partial(join_body, capacity, len(parts)),
        jax.ShapeDtypeStruct(shape, parts[0].dtype),
        "join",
        0,
        4 * shape[0] * shape[1],
        [pl.BlockSpec(memory_space=pltpu.VMEM)] * (len(parts) + len(after)),
    )(*shuffled(parts, True), *after)


def expert_body(group, capacity, experts, spare, layers, up_ref, down_ref, *refs):
    refs = list(refs)
    if spare:
        place_ref = refs.pop(0)
    batch_refs = refs[:group]
    out_refs = refs[group : 2 * group]
    features, hidden_width = up_ref.shape[1:]
    block = batch_refs[0].shape[0] // STREAMS
    for stream in range(STREAMS):
        mine = slice(stream * block, (stream + 1) * block)
        rows = jnp.concatenate([ref[mine, :features] for ref in batch_refs])
        raw = jnp.dot(rows, up_ref[stream], preferred_element_type=jnp.float32)
        hidden = jax.nn.silu(raw).astype(jnp.bfloat16)
        value = jnp.dot(hidden, down_ref[stream], preferred_element_type=jnp.float32)
        for h in range(group):
            out_refs[h][mine, :] = value[h * block : (h + 1) * block].astype(jnp.bfloat16)
    if spare:
        table_ref = refs[2 * group]
        place = place_ref[0, 1]
        rows = table_ref.shape[0]
        at = lane_ids(1, spare) % experts
        lanes = lane_ids(rows)
        ladder = lax.broadcasted_iota(jnp.int32, (rows, LANES), 0)
        table = jnp.zeros((rows, LANES), jnp.float32)
        for stream in range(STREAMS):
            total = jnp.zeros((1, spare), jnp.float32)
            for ref in batch_refs:
                values = ref[:, features:].astype(jnp.float32)
                for k in range(experts):
                    row = stream * block + k * capacity
                    total = total + values[row : row + 1]
            row = place if stream == 0 else layers - 1 - place
            for e in range(experts):
                value = jnp.sum(jnp.where(at == e, total, 0.0), axis=1, keepdims=True)
                table = table + jnp.where((ladder == row) & (lanes == e), value, 0.0)
        table_ref[...] = table


def expert_rows(batch, up, down, capacity, experts, spare, place=None, layers=0):
    group = len(batch)
    features, hidden_width = up.shape[1:]
    rows = batch[0].shape[0]
    outs = [jax.ShapeDtypeStruct((rows, features), jnp.bfloat16) for _ in range(group)]
    inputs = [in_vmem(up), in_vmem(down)]
    if spare:
        outs.append(jax.ShapeDtypeStruct((-(-layers // TABLE_ROWS) * TABLE_ROWS, LANES), jnp.float32))
        inputs.append(place)
    inputs += batch
    in_place = pl.BlockSpec(memory_space=pltpu.VMEM)
    return call(
        functools.partial(expert_body, group, capacity, experts, spare, layers),
        outs,
        "experts",
        4 * group * rows * features * hidden_width,
        2 * up.size,
        [in_place] * len(inputs),
    )(*inputs)


def add_body(experts, capacity, *refs):
    parts = refs[:-experts]
    summed = sum(part[...].astype(jnp.float32) for part in parts)
    block = summed.shape[0] // STREAMS
    for k in range(experts):
        refs[len(parts) + k][...] = jnp.concatenate(
            [
                summed[stream * block + k * capacity : stream * block + (k + 1) * capacity]
                for stream in range(STREAMS)
            ]
        ).astype(jnp.bfloat16)


def add_up(parts, experts, capacity, held=()):
    rows, features = parts[0].shape
    outs = [
        jax.ShapeDtypeStruct((rows // experts, features), jnp.bfloat16) for _ in range(experts)
    ]
    return call(
        functools.partial(add_body, experts, capacity),
        outs,
        "add_up",
        0,
        4 * rows * features,
        inputs=len(parts),
        held=held,
    )(*parts)


def finish_body(experts, capacity, scale, x_ref, me_ref, coefficient_ref, *refs):
    parts = [ref[...].astype(jnp.float32) for ref in arranged(refs[:experts], False)]
    rest = refs[experts:]
    results = []
    for stream in range(STREAMS):
        returned = jnp.concatenate(
            [part[stream * capacity : (stream + 1) * capacity] for part in parts]
        ).astype(jnp.bfloat16)
        coefficient = coefficient_ref[stream, :, : experts * capacity]
        high = coefficient.astype(jnp.bfloat16)
        low = (coefficient - high.astype(jnp.float32)).astype(jnp.bfloat16)
        mixture = jnp.dot(high, returned, preferred_element_type=jnp.float32) + jnp.dot(
            low, returned, preferred_element_type=jnp.float32
        )
        results.append(x_ref[stream].astype(jnp.float32) + mixture)
    if not scale:
        even = is_even(me_ref[0, 1], mixture.shape)
        results = [
            jnp.where(even, results[1], results[0]),
            jnp.where(even, results[0], results[1]),
        ]
    for out_ref, result in zip(rest[-STREAMS - 1 :] if scale else rest, results):
        out_ref[...] = result.astype(out_ref.dtype)
    if scale:
        layers = rest[-1].shape[0]
        table = sum(ref[:layers, :] for ref in rest[: -STREAMS - 1])
        rest[-1][...] = table[:, :experts] / scale


def finish(x, me, coefficient, parts, capacity, layers, tables=(), scale=0.0, held=()):
    experts = len(parts)
    rows, features = coefficient.shape[1], parts[0].shape[1]
    outs = [jax.ShapeDtypeStruct((rows, features), jnp.bfloat16) for _ in range(STREAMS)]
    if scale:
        outs.append(jax.ShapeDtypeStruct((layers, experts), jnp.float32))
    return call(
        functools.partial(finish_body, experts, capacity, scale),
        outs,
        "finish",
        128 * rows * features,
        12 * rows * features,
        inputs=3 + experts + len(tables),
        held=held,
    )(x, me, coefficient, *shuffled(parts, False), *tables)


class Ring:
    def __init__(self, experts):
        self.pipe = lax.axis_size("pipe")
        self.size = lax.axis_size("expert")
        self.experts = experts
        self.group = self.size // experts

    def across(self, blocks):
        moved = {0: blocks[0]}
        for k in sorted(range(1, self.experts), key=lambda k: -k):
            moved[k] = lax.ppermute(
                blocks[k], "expert", [(j, j ^ (k * self.group)) for j in range(self.size)]
            )
        return [moved[k] for k in range(self.experts)]

    def within(self, array, shift):
        pairs = [
            (j, j // self.group * self.group + (j + shift) % self.group) for j in range(self.size)
        ]
        return lax.ppermute(array, "expert", pairs)

    def far(self, array):
        steps = [(i + 1 if i % 2 else i - 1) % self.pipe for i in range(self.pipe)]
        return lax.ppermute(array, "pipe", list(enumerate(steps)))

    def near(self, array):
        return lax.ppermute(array, "pipe", [(i, i ^ 1) for i in range(self.pipe)])

    def over_sections(self, table):
        if self.pipe & (self.pipe - 1):
            return [lax.psum(table, "pipe")]
        parts = [table]
        step = 1
        while step < self.pipe:
            table = sum(parts[1:], parts[0])[: table.shape[0] if step == 1 else self.pipe]
            moved = lax.ppermute(table, "pipe", [(i, i ^ step) for i in range(self.pipe)])
            parts = [table, moved]
            step *= 2
        return parts


def shards(stream_a, stream_b, routes, up_weight, down_weight, router_weight):
    experts = router_weight.shape[-1]
    ring = Ring(experts)
    rows, features = stream_a.shape[1:]
    capacity = rows * routes.shape[-1] // experts
    me = jnp.stack([lax.axis_index("expert"), lax.axis_index("pipe")]).astype(jnp.int32)[None]
    router = jnp.swapaxes(router_weight[:, 0], 1, 2)
    picks = jnp.swapaxes(routes[:, :, 0], 2, 3)
    spare = -(-2 * experts * ring.size // LANES) * LANES
    tokens_total = 2 * TICKS * rows * ring.size
    up, down = up_weight[:, 0], down_weight[:, 0]
    held = ()
    for step in range(TICKS):
        first, last = step == 0, step == TICKS - 1
        room = spare if last else 0
        if first:
            blocks, others = prepare(
                [stream_a[0], stream_b[0], router, picks, me], ring.group, capacity
            )
            x, normed, slots, router, picks = others
            coefficient, mass, slots = gates(
                normed, slots, router, picks, me, ring.group, capacity, spare
            )
        else:
            blocks, (x, coefficient) = repeat(
                [*moved, slots, router, picks, mass, me], ring.group, capacity, spare, held
            )
        own = join(
            ring.across(blocks),
            capacity,
            [in_vmem(value) for value in held],
        )
        batch = [own] + [ring.within(own, h) for h in range(1, ring.group)]
        values = expert_rows(batch, up, down, capacity, experts, room, me, ring.pipe)
        held = () if last else (up, down)
        back = add_up(
            [values[0]] + [ring.within(values[h], -h) for h in range(1, ring.group)],
            experts,
            capacity,
            held,
        )
        tables = ring.over_sections(values[-1]) if last else ()
        result = finish(
            x,
            me,
            coefficient,
            ring.across(back),
            capacity,
            ring.pipe,
            tables,
            float(tokens_total) if last else 0.0,
            held,
        )
        if not last:
            moved = [ring.far(result[0]), ring.near(result[1])]
    return (result[0][None], result[1][None], result[2])


def solution(mesh):
    return jax.shard_map(
        shards,
        mesh=mesh,
        in_specs=(
            P("pipe", "expert", None),
            P("pipe", "expert", None),
            P(None, None, "pipe", "expert", None),
            P(None, "pipe", None, "expert"),
            P(None, "pipe", "expert", None),
            P(None, "pipe", None, None),
        ),
        out_specs=(P("pipe", "expert", None), P("pipe", "expert", None), P()),
        check_vma=False,
    )
```

```python
import functools

import jax
import jax.numpy as jnp
from jax import lax
from jax.experimental import pallas as pl
from jax.experimental.pallas import tpu as pltpu
from jax.sharding import PartitionSpec as P

TICKS = 2


EPS = 1e-06

LANES = 128

STREAMS = 2

EARLY_FLOPS = 2 * 10**10

TABLE_ROWS = 64


def in_hbm(array):
    return pltpu.with_memory_space_constraint(array, pltpu.HBM)


def in_vmem(array):
    return pltpu.with_memory_space_constraint(array, pltpu.VMEM)


def call(
    body, outs, name, flops=0, size=0, in_specs=None, out_specs=None, scratch=(), inputs=0, held=()
):
    more = {}
    if held:
        in_specs = [pl.BlockSpec(memory_space=pltpu.VMEM)] * (inputs + len(held))

        def whole_body(*refs):
            body(*refs[:inputs], *refs[inputs + len(held) :])

        result = call(whole_body, outs, name, flops, size, in_specs, out_specs, scratch)
        return lambda *operands: result(*operands, *[in_vmem(value) for value in held])
    if in_specs is not None:
        more["in_specs"] = in_specs
    if out_specs is not None:
        more["out_specs"] = out_specs
    return pl.pallas_call(
        body,
        out_shape=outs,
        name=name,
        scratch_shapes=scratch,
        cost_estimate=pl.CostEstimate(flops=flops, bytes_accessed=size, transcendentals=0),
        compiler_params=pltpu.CompilerParams(vmem_limit_bytes=8 << 20),
        **more,
    )


def lane_ids(rows, width=LANES):
    return lax.broadcasted_iota(jnp.int32, (rows, width), 1)


def is_even(place, shape):
    return (lax.broadcasted_iota(jnp.int32, shape, 0) * 0 + place) % 2 == 0


def upright(row):
    n = row.shape[1]
    square = jnp.broadcast_to(row, (n, n))
    diagonal = lax.broadcasted_iota(jnp.int32, (n, n), 0) == lax.broadcasted_iota(
        jnp.int32, (n, n), 1
    )
    return jnp.sum(jnp.where(diagonal, square, 0.0), axis=1, keepdims=True)


def normalize(x):
    wide = x.astype(jnp.float32)
    return (wide * lax.rsqrt(jnp.mean(wide * wide, axis=-1, keepdims=True) + EPS)).astype(
        jnp.bfloat16
    )


def chosen_by(picks):
    return [upright(picks[i : i + 1, :].astype(jnp.float32)).astype(jnp.int32) for i in range(2)]


def place_rows(chosen, mine, rows, capacity):
    lanes = lane_ids(rows)
    rows_at = lax.broadcasted_iota(jnp.int32, (rows, LANES), 0)
    kind = lanes // capacity
    named = ((chosen[0] ^ mine) == kind) | ((chosen[1] ^ mine) == kind)
    named_f = jnp.where(named, 1.0, 0.0)
    before = jnp.zeros((rows, LANES), jnp.float32)
    for r in range(rows - 1):
        before = before + jnp.where(rows_at > r, named_f[r : r + 1, :], 0.0)
    slot = named & (before == (lanes % capacity).astype(jnp.float32))
    return jnp.where(slot, 1.0, 0.0)


def pack_rows(place, normed, slots):
    return jnp.dot(
        place.T[:slots].astype(jnp.bfloat16), normed, preferred_element_type=jnp.float32
    )


def gate_rows(normed, router, chosen, place, me, mine, experts, capacity, spare):
    rows = normed.shape[0]
    wide = normed.astype(jnp.float32)
    taken = [jnp.zeros((rows, 1), jnp.float32) for _ in range(2)]
    for e in range(experts):
        affinity = jax.nn.sigmoid(
            jnp.sum(wide * router[e : e + 1, :].astype(jnp.float32), axis=1, keepdims=True)
        )
        taken = [jnp.where(pick == e, affinity, old) for pick, old in zip(chosen, taken)]
    whole = taken[0] + taken[1]
    shares = [taken[0] / whole, taken[1] / whole]
    kind = lane_ids(rows) // capacity
    share_at = jnp.where((chosen[0] ^ mine) == kind, shares[0], 0.0) + jnp.where(
        (chosen[1] ^ mine) == kind, shares[1], 0.0
    )
    spread = lane_ids(rows, spare)
    masses = []
    for shift in (0, experts):
        base = me * 2 * experts + shift
        here = jnp.where(spread == chosen[0] + base, shares[0], 0.0)
        here = here + jnp.where(spread == chosen[1] + base, shares[1], 0.0)
        masses.append(jnp.sum(here, axis=0, keepdims=True))
    return place * share_at, jnp.concatenate(masses)


def carry_masses(masses):
    top = masses.astype(jnp.bfloat16).astype(jnp.float32)
    return top[:1] + (masses - top)[1:]


def store_blocks(packed, block_refs, capacity):
    features = packed[0].shape[1]
    for k, block_ref in enumerate(block_refs):
        rows = [part[k * capacity : (k + 1) * capacity] for part in packed]
        block_ref[:, :features] = jnp.concatenate(rows).astype(jnp.bfloat16)


def prepare_body(group, experts, capacity, *refs):
    sources, me_ref = refs[:4], refs[4]
    block_refs = refs[5 : 5 + experts]
    x_ref, normed_ref, place_ref, router_ref, routes_ref, sems = refs[5 + experts :]
    targets = [x_ref.at[0], x_ref.at[1], router_ref, routes_ref]
    copies = [
        pltpu.make_async_copy(source, target, sems.at[i])
        for i, (source, target) in enumerate(zip(sources, targets))
    ]
    for copy in copies:
        copy.start()
    mine = lax.div(me_ref[0, 0], group)
    rows = x_ref.shape[1]
    copies[3].wait()
    places = [
        place_rows(chosen_by(routes_ref[0, stream]), mine, rows, capacity)
        for stream in range(STREAMS)
    ]
    for copy in copies[:3]:
        copy.wait()
    packed = []
    for stream in range(STREAMS):
        normed = normalize(x_ref[stream])
        normed_ref[stream] = normed
        place_ref[stream] = places[stream]
        packed.append(pack_rows(places[stream], normed, experts * capacity))
    store_blocks(packed, block_refs, capacity)


def prepare(inputs, group, capacity):
    x, _, router, routes, _ = inputs
    rows, features = x.shape
    experts = router.shape[1]
    both = jax.ShapeDtypeStruct((STREAMS, rows, features), jnp.bfloat16)
    outs = [
        jax.ShapeDtypeStruct((STREAMS * capacity, features), jnp.bfloat16) for _ in range(experts)
    ]
    outs += [
        both,
        both,
        jax.ShapeDtypeStruct((STREAMS, rows, LANES), jnp.float32),
        jax.ShapeDtypeStruct(router.shape, router.dtype),
        jax.ShapeDtypeStruct(routes.shape, routes.dtype),
    ]
    result = call(
        functools.partial(prepare_body, group, experts, capacity),
        outs,
        "prepare",
        EARLY_FLOPS,
        4 * rows * features,
        [pl.BlockSpec(memory_space=pl.ANY)] * 4 + [pl.BlockSpec(memory_space=pltpu.VMEM)],
        None,
        [pltpu.SemaphoreType.DMA((4,))],
    )(*[in_hbm(value) for value in inputs[:4]], inputs[4])
    return result[:experts], result[experts:]


def gates_body(group, experts, capacity, spare, *refs):
    normed_ref, place_ref, router_ref, routes_ref, me_ref = refs[:5]
    coefficient_ref, mass_ref, next_ref = refs[5:]
    me = me_ref[0, 0]
    mine = lax.div(me, group)
    rows = normed_ref.shape[1]
    for stream in range(STREAMS):
        coefficient_ref[stream], mass_ref[stream] = gate_rows(
            normed_ref[stream],
            router_ref[stream],
            chosen_by(routes_ref[0, stream]),
            place_ref[stream],
            me,
            mine,
            experts,
            capacity,
            spare,
        )
        next_ref[stream] = place_rows(chosen_by(routes_ref[1, stream]), mine, rows, capacity)


def gates(normed, place, router, routes, me, group, capacity, spare):
    experts = router.shape[1]
    outs = [
        jax.ShapeDtypeStruct(place.shape, jnp.float32),
        jax.ShapeDtypeStruct((STREAMS, 2, spare), jnp.float32),
        jax.ShapeDtypeStruct(place.shape, jnp.float32),
    ]
    return call(
        functools.partial(gates_body, group, experts, capacity, spare),
        outs,
        "gates",
        32 * normed.size,
        4 * normed.size,
    )(normed, place, router, routes, me)


def repeat_body(group, experts, capacity, spare, *refs):
    far_ref, near_ref, place_ref, router_ref, routes_ref, old_ref, me_ref = refs[:7]
    block_refs = refs[7 : 7 + experts]
    x_ref, coefficient_ref = refs[7 + experts :]
    me = me_ref[0, 0]
    mine = lax.div(me, group)
    far, near = far_ref[...], near_ref[...]
    features = near.shape[1]
    even = is_even(me_ref[0, 1], near.shape)
    xs = [jnp.where(even, far, near), jnp.where(even, near, far)]
    packed, carried = [], []
    for stream in range(STREAMS):
        x_ref[stream] = xs[stream]
        normed = normalize(xs[stream])
        packed.append(pack_rows(place_ref[stream], normed, experts * capacity))
        coefficient, masses = gate_rows(
            normed,
            router_ref[stream],
            chosen_by(routes_ref[1, stream]),
            place_ref[stream],
            me,
            mine,
            experts,
            capacity,
            spare,
        )
        coefficient_ref[stream] = coefficient
        carried.append(
            jnp.broadcast_to(carry_masses(masses + old_ref[stream]), (capacity, spare))
        )
    store_blocks(packed, block_refs, capacity)
    carried = jnp.concatenate(carried).astype(jnp.bfloat16)
    for block_ref in block_refs:
        block_ref[:, features:] = carried


def repeat(inputs, group, capacity, spare, held):
    near, place, router = inputs[1:4]
    rows, features = near.shape
    experts = router.shape[1]
    outs = [
        jax.ShapeDtypeStruct((STREAMS * capacity, features + spare), jnp.bfloat16)
        for _ in range(experts)
    ]
    outs += [
        jax.ShapeDtypeStruct((STREAMS, rows, features), jnp.bfloat16),
        jax.ShapeDtypeStruct(place.shape, jnp.float32),
    ]
    result = call(
        functools.partial(repeat_body, group, experts, capacity, spare),
        outs,
        "prepare",
        512 * rows * features,
        4 * rows * features,
        inputs=len(inputs),
        held=held,
    )(*inputs)
    return result[:experts], result[experts:]


def order_of(experts, out):
    return [0, *range(2, experts), 1] if out else [0, *range(experts - 1, 0, -1)]


def shuffled(parts, out):
    return [parts[k] for k in order_of(len(parts), out)]


def arranged(parts, out):
    order = order_of(len(parts), out)
    return [parts[order.index(k)] for k in range(len(parts))]


def join_body(capacity, experts, *refs):
    parts, out_ref = arranged(refs[:experts], True), refs[-1]
    rows = [part[...].astype(jnp.float32) for part in parts]
    out_ref[...] = jnp.concatenate(
        [
            part[stream * capacity : (stream + 1) * capacity]
            for stream in range(STREAMS)
            for part in rows
        ]
    ).astype(out_ref.dtype)


def join(parts, capacity, after=()):
    shape = (sum(part.shape[0] for part in parts), parts[0].shape[1])
    return call(
        functools.partial(join_body, capacity, len(parts)),
        jax.ShapeDtypeStruct(shape, parts[0].dtype),
        "join",
        0,
        4 * shape[0] * shape[1],
        [pl.BlockSpec(memory_space=pltpu.VMEM)] * (len(parts) + len(after)),
    )(*shuffled(parts, True), *after)


def expert_body(group, capacity, experts, spare, layers, up_ref, down_ref, *refs):
    refs = list(refs)
    if spare:
        place_ref = refs.pop(0)
    batch_refs = refs[:group]
    out_refs = refs[group : 2 * group]
    features, hidden_width = up_ref.shape[1:]
    block = batch_refs[0].shape[0] // STREAMS
    hidden = []
    for stream in range(STREAMS):
        mine = slice(stream * block, (stream + 1) * block)
        rows = jnp.concatenate([ref[mine, :features] for ref in batch_refs])
        raw = jnp.dot(rows, up_ref[stream], preferred_element_type=jnp.float32)
        hidden.append(jax.nn.silu(raw).astype(jnp.bfloat16))
    for stream in range(STREAMS):
        mine = slice(stream * block, (stream + 1) * block)
        value = jnp.dot(hidden[stream], down_ref[stream], preferred_element_type=jnp.float32)
        for h in range(group):
            out_refs[h][mine, :] = value[h * block : (h + 1) * block].astype(jnp.bfloat16)
    if spare:
        table_ref = refs[2 * group]
        place = place_ref[0, 1]
        rows = table_ref.shape[0]
        at = lane_ids(1, spare) % experts
        lanes = lane_ids(rows)
        ladder = lax.broadcasted_iota(jnp.int32, (rows, LANES), 0)
        table = jnp.zeros((rows, LANES), jnp.float32)
        for stream in range(STREAMS):
            total = jnp.zeros((1, spare), jnp.float32)
            for ref in batch_refs:
                values = ref[:, features:].astype(jnp.float32)
                for k in range(experts):
                    row = stream * block + k * capacity
                    total = total + values[row : row + 1]
            row = place if stream == 0 else layers - 1 - place
            for e in range(experts):
                value = jnp.sum(jnp.where(at == e, total, 0.0), axis=1, keepdims=True)
                table = table + jnp.where((ladder == row) & (lanes == e), value, 0.0)
        table_ref[...] = table


def expert_rows(batch, up, down, capacity, experts, spare, place=None, layers=0):
    group = len(batch)
    features, hidden_width = up.shape[1:]
    rows = batch[0].shape[0]
    outs = [jax.ShapeDtypeStruct((rows, features), jnp.bfloat16) for _ in range(group)]
    inputs = [in_vmem(up), in_vmem(down)]
    if spare:
        outs.append(jax.ShapeDtypeStruct((-(-layers // TABLE_ROWS) * TABLE_ROWS, LANES), jnp.float32))
        inputs.append(place)
    inputs += batch
    in_place = pl.BlockSpec(memory_space=pltpu.VMEM)
    return call(
        functools.partial(expert_body, group, capacity, experts, spare, layers),
        outs,
        "experts",
        4 * group * rows * features * hidden_width,
        2 * up.size,
        [in_place] * len(inputs),
    )(*inputs)


def add_body(experts, capacity, *refs):
    parts = refs[:-experts]
    summed = sum(part[...].astype(jnp.float32) for part in parts)
    block = summed.shape[0] // STREAMS
    for k in range(experts):
        refs[len(parts) + k][...] = jnp.concatenate(
            [
                summed[stream * block + k * capacity : stream * block + (k + 1) * capacity]
                for stream in range(STREAMS)
            ]
        ).astype(jnp.bfloat16)


def add_up(parts, experts, capacity, held=()):
    rows, features = parts[0].shape
    outs = [
        jax.ShapeDtypeStruct((rows // experts, features), jnp.bfloat16) for _ in range(experts)
    ]
    return call(
        functools.partial(add_body, experts, capacity),
        outs,
        "add_up",
        0,
        4 * rows * features,
        inputs=len(parts),
        held=held,
    )(*parts)


def finish_body(experts, capacity, scale, x_ref, me_ref, coefficient_ref, *refs):
    parts = [ref[...].astype(jnp.float32) for ref in arranged(refs[:experts], False)]
    rest = refs[experts:]
    results = []
    for stream in range(STREAMS):
        returned = jnp.concatenate(
            [part[stream * capacity : (stream + 1) * capacity] for part in parts]
        ).astype(jnp.bfloat16)
        coefficient = coefficient_ref[stream, :, : experts * capacity]
        high = coefficient.astype(jnp.bfloat16)
        low = (coefficient - high.astype(jnp.float32)).astype(jnp.bfloat16)
        mixture = jnp.dot(high, returned, preferred_element_type=jnp.float32) + jnp.dot(
            low, returned, preferred_element_type=jnp.float32
        )
        results.append(x_ref[stream].astype(jnp.float32) + mixture)
    if not scale:
        even = is_even(me_ref[0, 1], mixture.shape)
        results = [
            jnp.where(even, results[1], results[0]),
            jnp.where(even, results[0], results[1]),
        ]
    for out_ref, result in zip(rest[-STREAMS - 1 :] if scale else rest, results):
        out_ref[...] = result.astype(out_ref.dtype)
    if scale:
        layers = rest[-1].shape[0]
        table = sum(ref[:layers, :] for ref in rest[: -STREAMS - 1])
        rest[-1][...] = table[:, :experts] / scale


def finish(x, me, coefficient, parts, capacity, layers, tables=(), scale=0.0, held=()):
    experts = len(parts)
    rows, features = coefficient.shape[1], parts[0].shape[1]
    outs = [jax.ShapeDtypeStruct((rows, features), jnp.bfloat16) for _ in range(STREAMS)]
    if scale:
        outs.append(jax.ShapeDtypeStruct((layers, experts), jnp.float32))
    return call(
        functools.partial(finish_body, experts, capacity, scale),
        outs,
        "finish",
        128 * rows * features,
        12 * rows * features,
        inputs=3 + experts + len(tables),
        held=held,
    )(x, me, coefficient, *shuffled(parts, False), *tables)


class Ring:
    def __init__(self, experts):
        self.pipe = lax.axis_size("pipe")
        self.size = lax.axis_size("expert")
        self.experts = experts
        self.group = self.size // experts

    def across(self, blocks):
        moved = {0: blocks[0]}
        for k in sorted(range(1, self.experts), key=lambda k: -k):
            moved[k] = lax.ppermute(
                blocks[k], "expert", [(j, j ^ (k * self.group)) for j in range(self.size)]
            )
        return [moved[k] for k in range(self.experts)]

    def within(self, array, shift):
        pairs = [
            (j, j // self.group * self.group + (j + shift) % self.group) for j in range(self.size)
        ]
        return lax.ppermute(array, "expert", pairs)

    def far(self, array):
        steps = [(i + 1 if i % 2 else i - 1) % self.pipe for i in range(self.pipe)]
        return lax.ppermute(array, "pipe", list(enumerate(steps)))

    def near(self, array):
        return lax.ppermute(array, "pipe", [(i, i ^ 1) for i in range(self.pipe)])

    def over_sections(self, table):
        if self.pipe & (self.pipe - 1):
            return [lax.psum(table, "pipe")]
        parts = [table]
        step = 1
        while step < self.pipe:
            table = sum(parts[1:], parts[0])[: table.shape[0] if step == 1 else self.pipe]
            moved = lax.ppermute(table, "pipe", [(i, i ^ step) for i in range(self.pipe)])
            parts = [table, moved]
            step *= 2
        return parts


def shards(stream_a, stream_b, routes, up_weight, down_weight, router_weight):
    experts = router_weight.shape[-1]
    ring = Ring(experts)
    rows, features = stream_a.shape[1:]
    capacity = rows * routes.shape[-1] // experts
    me = jnp.stack([lax.axis_index("expert"), lax.axis_index("pipe")]).astype(jnp.int32)[None]
    router = jnp.swapaxes(router_weight[:, 0], 1, 2)
    picks = jnp.swapaxes(routes[:, :, 0], 2, 3)
    spare = -(-2 * experts * ring.size // LANES) * LANES
    tokens_total = 2 * TICKS * rows * ring.size
    up, down = up_weight[:, 0], down_weight[:, 0]
    held = ()
    for step in range(TICKS):
        first, last = step == 0, step == TICKS - 1
        room = spare if last else 0
        if first:
            blocks, others = prepare(
                [stream_a[0], stream_b[0], router, picks, me], ring.group, capacity
            )
            x, normed, slots, router, picks = others
            coefficient, mass, slots = gates(
                normed, slots, router, picks, me, ring.group, capacity, spare
            )
        else:
            blocks, (x, coefficient) = repeat(
                [*moved, slots, router, picks, mass, me], ring.group, capacity, spare, held
            )
        own = join(
            ring.across(blocks),
            capacity,
            [in_vmem(value) for value in held],
        )
        batch = [own] + [ring.within(own, h) for h in range(1, ring.group)]
        values = expert_rows(batch, up, down, capacity, experts, room, me, ring.pipe)
        held = () if last else (up, down)
        back = add_up(
            [values[0]] + [ring.within(values[h], -h) for h in range(1, ring.group)],
            experts,
            capacity,
            held,
        )
        tables = ring.over_sections(values[-1]) if last else ()
        result = finish(
            x,
            me,
            coefficient,
            ring.across(back),
            capacity,
            ring.pipe,
            tables,
            float(tokens_total) if last else 0.0,
            held,
        )
        if not last:
            moved = [ring.far(result[0]), ring.near(result[1])]
    return (result[0][None], result[1][None], result[2])


def solution(mesh):
    return jax.shard_map(
        shards,
        mesh=mesh,
        in_specs=(
            P("pipe", "expert", None),
            P("pipe", "expert", None),
            P(None, None, "pipe", "expert", None),
            P(None, "pipe", None, "expert"),
            P(None, "pipe", "expert", None),
            P(None, "pipe", None, None),
        ),
        out_specs=(P("pipe", "expert", None), P("pipe", "expert", None), P()),
        check_vma=False,
    )
```

```python
import functools

import jax
import jax.numpy as jnp
from jax import lax
from jax.experimental import pallas as pl
from jax.experimental.pallas import tpu as pltpu
from jax.sharding import PartitionSpec as P

TICKS = 2


EPS = 1e-06

LANES = 128

STREAMS = 2

EARLY_FLOPS = 2 * 10**10

TABLE_ROWS = 64


def in_hbm(array):
    return pltpu.with_memory_space_constraint(array, pltpu.HBM)


def in_vmem(array):
    return pltpu.with_memory_space_constraint(array, pltpu.VMEM)


def call(
    body, outs, name, flops=0, size=0, in_specs=None, out_specs=None, scratch=(), inputs=0, held=()
):
    more = {}
    if held:
        in_specs = [pl.BlockSpec(memory_space=pltpu.VMEM)] * (inputs + len(held))

        def whole_body(*refs):
            body(*refs[:inputs], *refs[inputs + len(held) :])

        result = call(whole_body, outs, name, flops, size, in_specs, out_specs, scratch)
        return lambda *operands: result(*operands, *[in_vmem(value) for value in held])
    if in_specs is not None:
        more["in_specs"] = in_specs
    if out_specs is not None:
        more["out_specs"] = out_specs
    return pl.pallas_call(
        body,
        out_shape=outs,
        name=name,
        scratch_shapes=scratch,
        cost_estimate=pl.CostEstimate(flops=flops, bytes_accessed=size, transcendentals=0),
        compiler_params=pltpu.CompilerParams(vmem_limit_bytes=8 << 20),
        **more,
    )


def lane_ids(rows, width=LANES):
    return lax.broadcasted_iota(jnp.int32, (rows, width), 1)


def is_even(place, shape):
    return (lax.broadcasted_iota(jnp.int32, shape, 0) * 0 + place) % 2 == 0


def upright(row):
    n = row.shape[1]
    square = jnp.broadcast_to(row, (n, n))
    diagonal = lax.broadcasted_iota(jnp.int32, (n, n), 0) == lax.broadcasted_iota(
        jnp.int32, (n, n), 1
    )
    return jnp.sum(jnp.where(diagonal, square, 0.0), axis=1, keepdims=True)


def normalize(x):
    wide = x.astype(jnp.float32)
    return (wide * lax.rsqrt(jnp.mean(wide * wide, axis=-1, keepdims=True) + EPS)).astype(
        jnp.bfloat16
    )


def chosen_by(picks):
    return [upright(picks[i : i + 1, :].astype(jnp.float32)).astype(jnp.int32) for i in range(2)]


def place_rows(chosen, mine, rows, capacity):
    lanes = lane_ids(rows)
    rows_at = lax.broadcasted_iota(jnp.int32, (rows, LANES), 0)
    kind = lanes // capacity
    named = ((chosen[0] ^ mine) == kind) | ((chosen[1] ^ mine) == kind)
    named_f = jnp.where(named, 1.0, 0.0)
    before = jnp.zeros((rows, LANES), jnp.float32)
    for r in range(rows - 1):
        before = before + jnp.where(rows_at > r, named_f[r : r + 1, :], 0.0)
    slot = named & (before == (lanes % capacity).astype(jnp.float32))
    return jnp.where(slot, 1.0, 0.0)


def turned(place, slots):
    return place.T[:slots].astype(jnp.bfloat16)


def pack_rows(turned_place, normed):
    return jnp.dot(turned_place, normed, preferred_element_type=jnp.float32)


def gate_rows(normed, router, chosen, place, me, mine, experts, capacity, spare):
    rows = normed.shape[0]
    wide = normed.astype(jnp.float32)
    taken = [jnp.zeros((rows, 1), jnp.float32) for _ in range(2)]
    for e in range(experts):
        affinity = jax.nn.sigmoid(
            jnp.sum(wide * router[e : e + 1, :].astype(jnp.float32), axis=1, keepdims=True)
        )
        taken = [jnp.where(pick == e, affinity, old) for pick, old in zip(chosen, taken)]
    whole = taken[0] + taken[1]
    shares = [taken[0] / whole, taken[1] / whole]
    kind = lane_ids(rows) // capacity
    share_at = jnp.where((chosen[0] ^ mine) == kind, shares[0], 0.0) + jnp.where(
        (chosen[1] ^ mine) == kind, shares[1], 0.0
    )
    spread = lane_ids(rows, spare)
    masses = []
    for shift in (0, experts):
        base = me * 2 * experts + shift
        here = jnp.where(spread == chosen[0] + base, shares[0], 0.0)
        here = here + jnp.where(spread == chosen[1] + base, shares[1], 0.0)
        masses.append(jnp.sum(here, axis=0, keepdims=True))
    return place * share_at, jnp.concatenate(masses)


def carry_masses(masses):
    top = masses.astype(jnp.bfloat16).astype(jnp.float32)
    return top[:1] + (masses - top)[1:]


def store_blocks(packed, block_refs, capacity):
    features = packed[0].shape[1]
    for k, block_ref in enumerate(block_refs):
        rows = [part[k * capacity : (k + 1) * capacity] for part in packed]
        block_ref[:, :features] = jnp.concatenate(rows).astype(jnp.bfloat16)


def prepare_body(group, experts, capacity, *refs):
    sources, me_ref = refs[:4], refs[4]
    block_refs = refs[5 : 5 + experts]
    x_ref, normed_ref, place_ref, router_ref, routes_ref, sems = refs[5 + experts :]
    targets = [x_ref.at[0], x_ref.at[1], router_ref, routes_ref]
    copies = [
        pltpu.make_async_copy(source, target, sems.at[i])
        for i, (source, target) in enumerate(zip(sources, targets))
    ]
    for copy in copies:
        copy.start()
    mine = lax.div(me_ref[0, 0], group)
    rows = x_ref.shape[1]
    copies[3].wait()
    places = [
        place_rows(chosen_by(routes_ref[0, stream]), mine, rows, capacity)
        for stream in range(STREAMS)
    ]
    for copy in copies[:3]:
        copy.wait()
    packed = []
    for stream in range(STREAMS):
        normed = normalize(x_ref[stream])
        normed_ref[stream] = normed
        place_ref[stream] = places[stream]
        packed.append(pack_rows(turned(places[stream], experts * capacity), normed))
    store_blocks(packed, block_refs, capacity)


def prepare(inputs, group, capacity):
    x, _, router, routes, _ = inputs
    rows, features = x.shape
    experts = router.shape[1]
    both = jax.ShapeDtypeStruct((STREAMS, rows, features), jnp.bfloat16)
    outs = [
        jax.ShapeDtypeStruct((STREAMS * capacity, features), jnp.bfloat16) for _ in range(experts)
    ]
    outs += [
        both,
        both,
        jax.ShapeDtypeStruct((STREAMS, rows, LANES), jnp.float32),
        jax.ShapeDtypeStruct(router.shape, router.dtype),
        jax.ShapeDtypeStruct(routes.shape, routes.dtype),
    ]
    result = call(
        functools.partial(prepare_body, group, experts, capacity),
        outs,
        "prepare",
        EARLY_FLOPS,
        4 * rows * features,
        [pl.BlockSpec(memory_space=pl.ANY)] * 4 + [pl.BlockSpec(memory_space=pltpu.VMEM)],
        None,
        [pltpu.SemaphoreType.DMA((4,))],
    )(*[in_hbm(value) for value in inputs[:4]], inputs[4])
    return result[:experts], result[experts:]


def gates_body(group, experts, capacity, spare, *refs):
    normed_ref, place_ref, router_ref, routes_ref, me_ref = refs[:5]
    coefficient_ref, mass_ref, next_ref, turned_ref = refs[5:]
    me = me_ref[0, 0]
    mine = lax.div(me, group)
    rows = normed_ref.shape[1]
    for stream in range(STREAMS):
        coefficient_ref[stream], mass_ref[stream] = gate_rows(
            normed_ref[stream],
            router_ref[stream],
            chosen_by(routes_ref[0, stream]),
            place_ref[stream],
            me,
            mine,
            experts,
            capacity,
            spare,
        )
        place = place_rows(chosen_by(routes_ref[1, stream]), mine, rows, capacity)
        next_ref[stream] = place
        turned_ref[stream] = turned(place, experts * capacity)


def gates(normed, place, router, routes, me, group, capacity, spare):
    experts = router.shape[1]
    outs = [
        jax.ShapeDtypeStruct(place.shape, jnp.float32),
        jax.ShapeDtypeStruct((STREAMS, 2, spare), jnp.float32),
        jax.ShapeDtypeStruct(place.shape, jnp.float32),
        jax.ShapeDtypeStruct((STREAMS, experts * capacity, place.shape[1]), jnp.bfloat16),
    ]
    return call(
        functools.partial(gates_body, group, experts, capacity, spare),
        outs,
        "gates",
        32 * normed.size,
        4 * normed.size,
    )(normed, place, router, routes, me)


def repeat_body(group, experts, capacity, spare, *refs):
    far_ref, near_ref, place_ref, router_ref, routes_ref, old_ref, me_ref, turned_ref = refs[:8]
    block_refs = refs[8 : 8 + experts]
    x_ref, coefficient_ref = refs[8 + experts :]
    me = me_ref[0, 0]
    mine = lax.div(me, group)
    far, near = far_ref[...], near_ref[...]
    features = near.shape[1]
    even = is_even(me_ref[0, 1], near.shape)
    xs = [jnp.where(even, far, near), jnp.where(even, near, far)]
    packed, carried = [], []
    for stream in range(STREAMS):
        x_ref[stream] = xs[stream]
        normed = normalize(xs[stream])
        packed.append(pack_rows(turned_ref[stream], normed))
        coefficient, masses = gate_rows(
            normed,
            router_ref[stream],
            chosen_by(routes_ref[1, stream]),
            place_ref[stream],
            me,
            mine,
            experts,
            capacity,
            spare,
        )
        coefficient_ref[stream] = coefficient
        carried.append(
            jnp.broadcast_to(carry_masses(masses + old_ref[stream]), (capacity, spare))
        )
    store_blocks(packed, block_refs, capacity)
    carried = jnp.concatenate(carried).astype(jnp.bfloat16)
    for block_ref in block_refs:
        block_ref[:, features:] = carried


def repeat(inputs, group, capacity, spare, held):
    near, place, router = inputs[1:4]
    rows, features = near.shape
    experts = router.shape[1]
    outs = [
        jax.ShapeDtypeStruct((STREAMS * capacity, features + spare), jnp.bfloat16)
        for _ in range(experts)
    ]
    outs += [
        jax.ShapeDtypeStruct((STREAMS, rows, features), jnp.bfloat16),
        jax.ShapeDtypeStruct(place.shape, jnp.float32),
    ]
    result = call(
        functools.partial(repeat_body, group, experts, capacity, spare),
        outs,
        "prepare",
        512 * rows * features,
        4 * rows * features,
        inputs=len(inputs),
        held=held,
    )(*inputs)
    return result[:experts], result[experts:]


def order_of(experts, out):
    return [0, *range(2, experts), 1] if out else [0, *range(experts - 1, 0, -1)]


def shuffled(parts, out):
    return [parts[k] for k in order_of(len(parts), out)]


def arranged(parts, out):
    order = order_of(len(parts), out)
    return [parts[order.index(k)] for k in range(len(parts))]


def join_body(capacity, experts, *refs):
    parts, out_ref = arranged(refs[:experts], True), refs[-1]
    rows = [part[...].astype(jnp.float32) for part in parts]
    out_ref[...] = jnp.concatenate(
        [
            part[stream * capacity : (stream + 1) * capacity]
            for stream in range(STREAMS)
            for part in rows
        ]
    ).astype(out_ref.dtype)


def join(parts, capacity, after=()):
    shape = (sum(part.shape[0] for part in parts), parts[0].shape[1])
    return call(
        functools.partial(join_body, capacity, len(parts)),
        jax.ShapeDtypeStruct(shape, parts[0].dtype),
        "join",
        0,
        4 * shape[0] * shape[1],
        [pl.BlockSpec(memory_space=pltpu.VMEM)] * (len(parts) + len(after)),
    )(*shuffled(parts, True), *after)


def expert_body(group, capacity, experts, spare, layers, up_ref, down_ref, *refs):
    refs = list(refs)
    if spare:
        place_ref = refs.pop(0)
    batch_refs = refs[:group]
    out_refs = refs[group : 2 * group]
    features, hidden_width = up_ref.shape[1:]
    block = batch_refs[0].shape[0] // STREAMS
    hidden = []
    for stream in range(STREAMS):
        mine = slice(stream * block, (stream + 1) * block)
        rows = jnp.concatenate([ref[mine, :features] for ref in batch_refs])
        raw = jnp.dot(rows, up_ref[stream], preferred_element_type=jnp.float32)
        hidden.append(jax.nn.silu(raw).astype(jnp.bfloat16))
    for stream in range(STREAMS):
        mine = slice(stream * block, (stream + 1) * block)
        value = jnp.dot(hidden[stream], down_ref[stream], preferred_element_type=jnp.float32)
        for h in range(group):
            out_refs[h][mine, :] = value[h * block : (h + 1) * block].astype(jnp.bfloat16)
    if spare:
        table_ref = refs[2 * group]
        place = place_ref[0, 1]
        rows = table_ref.shape[0]
        at = lane_ids(1, spare) % experts
        lanes = lane_ids(rows)
        ladder = lax.broadcasted_iota(jnp.int32, (rows, LANES), 0)
        table = jnp.zeros((rows, LANES), jnp.float32)
        for stream in range(STREAMS):
            total = jnp.zeros((1, spare), jnp.float32)
            for ref in batch_refs:
                values = ref[:, features:].astype(jnp.float32)
                for k in range(experts):
                    row = stream * block + k * capacity
                    total = total + values[row : row + 1]
            row = place if stream == 0 else layers - 1 - place
            for e in range(experts):
                value = jnp.sum(jnp.where(at == e, total, 0.0), axis=1, keepdims=True)
                table = table + jnp.where((ladder == row) & (lanes == e), value, 0.0)
        table_ref[...] = table


def expert_rows(batch, up, down, capacity, experts, spare, place=None, layers=0):
    group = len(batch)
    features, hidden_width = up.shape[1:]
    rows = batch[0].shape[0]
    outs = [jax.ShapeDtypeStruct((rows, features), jnp.bfloat16) for _ in range(group)]
    inputs = [in_vmem(up), in_vmem(down)]
    if spare:
        outs.append(jax.ShapeDtypeStruct((-(-layers // TABLE_ROWS) * TABLE_ROWS, LANES), jnp.float32))
        inputs.append(place)
    inputs += batch
    in_place = pl.BlockSpec(memory_space=pltpu.VMEM)
    return call(
        functools.partial(expert_body, group, capacity, experts, spare, layers),
        outs,
        "experts",
        4 * group * rows * features * hidden_width,
        2 * up.size,
        [in_place] * len(inputs),
    )(*inputs)


def add_body(experts, capacity, *refs):
    parts = refs[:-experts]
    summed = sum(part[...].astype(jnp.float32) for part in parts)
    block = summed.shape[0] // STREAMS
    for k in range(experts):
        refs[len(parts) + k][...] = jnp.concatenate(
            [
                summed[stream * block + k * capacity : stream * block + (k + 1) * capacity]
                for stream in range(STREAMS)
            ]
        ).astype(jnp.bfloat16)


def add_up(parts, experts, capacity, held=()):
    rows, features = parts[0].shape
    outs = [
        jax.ShapeDtypeStruct((rows // experts, features), jnp.bfloat16) for _ in range(experts)
    ]
    return call(
        functools.partial(add_body, experts, capacity),
        outs,
        "add_up",
        0,
        4 * rows * features,
        inputs=len(parts),
        held=held,
    )(*parts)


def finish_body(experts, capacity, scale, x_ref, me_ref, coefficient_ref, *refs):
    parts = [ref[...].astype(jnp.float32) for ref in arranged(refs[:experts], False)]
    rest = refs[experts:]
    results = []
    for stream in range(STREAMS):
        returned = jnp.concatenate(
            [part[stream * capacity : (stream + 1) * capacity] for part in parts]
        ).astype(jnp.bfloat16)
        coefficient = coefficient_ref[stream, :, : experts * capacity]
        high = coefficient.astype(jnp.bfloat16).astype(jnp.float32)
        halves = jnp.concatenate([high, coefficient - high]).astype(jnp.bfloat16)
        mixtures = jnp.dot(halves, returned, preferred_element_type=jnp.float32)
        rows = high.shape[0]
        mixture = mixtures[:rows] + mixtures[rows:]
        results.append(x_ref[stream].astype(jnp.float32) + mixture)
    if not scale:
        even = is_even(me_ref[0, 1], mixture.shape)
        results = [
            jnp.where(even, results[1], results[0]),
            jnp.where(even, results[0], results[1]),
        ]
    for out_ref, result in zip(rest[-STREAMS - 1 :] if scale else rest, results):
        out_ref[...] = result.astype(out_ref.dtype)
    if scale:
        layers = rest[-1].shape[0]
        table = sum(ref[:layers, :] for ref in rest[: -STREAMS - 1])
        rest[-1][...] = table[:, :experts] / scale


def finish(x, me, coefficient, parts, capacity, layers, tables=(), scale=0.0, held=()):
    experts = len(parts)
    rows, features = coefficient.shape[1], parts[0].shape[1]
    outs = [jax.ShapeDtypeStruct((rows, features), jnp.bfloat16) for _ in range(STREAMS)]
    if scale:
        outs.append(jax.ShapeDtypeStruct((layers, experts), jnp.float32))
    return call(
        functools.partial(finish_body, experts, capacity, scale),
        outs,
        "finish",
        128 * rows * features,
        12 * rows * features,
        inputs=3 + experts + len(tables),
        held=held,
    )(x, me, coefficient, *shuffled(parts, False), *tables)


class Ring:
    def __init__(self, experts):
        self.pipe = lax.axis_size("pipe")
        self.size = lax.axis_size("expert")
        self.experts = experts
        self.group = self.size // experts

    def across(self, blocks):
        moved = {0: blocks[0]}
        for k in sorted(range(1, self.experts), key=lambda k: -k):
            moved[k] = lax.ppermute(
                blocks[k], "expert", [(j, j ^ (k * self.group)) for j in range(self.size)]
            )
        return [moved[k] for k in range(self.experts)]

    def within(self, array, shift):
        pairs = [
            (j, j // self.group * self.group + (j + shift) % self.group) for j in range(self.size)
        ]
        return lax.ppermute(array, "expert", pairs)

    def far(self, array):
        steps = [(i + 1 if i % 2 else i - 1) % self.pipe for i in range(self.pipe)]
        return lax.ppermute(array, "pipe", list(enumerate(steps)))

    def near(self, array):
        return lax.ppermute(array, "pipe", [(i, i ^ 1) for i in range(self.pipe)])

    def over_sections(self, table):
        if self.pipe & (self.pipe - 1):
            return [lax.psum(table, "pipe")]
        parts = [table]
        step = 1
        while step < self.pipe:
            table = sum(parts[1:], parts[0])[: table.shape[0] if step == 1 else self.pipe]
            moved = lax.ppermute(table, "pipe", [(i, i ^ step) for i in range(self.pipe)])
            parts = [table, moved]
            step *= 2
        return parts


def shards(stream_a, stream_b, routes, up_weight, down_weight, router_weight):
    experts = router_weight.shape[-1]
    ring = Ring(experts)
    rows, features = stream_a.shape[1:]
    capacity = rows * routes.shape[-1] // experts
    me = jnp.stack([lax.axis_index("expert"), lax.axis_index("pipe")]).astype(jnp.int32)[None]
    router = jnp.swapaxes(router_weight[:, 0], 1, 2)
    picks = jnp.swapaxes(routes[:, :, 0], 2, 3)
    spare = -(-2 * experts * ring.size // LANES) * LANES
    tokens_total = 2 * TICKS * rows * ring.size
    up, down = up_weight[:, 0], down_weight[:, 0]
    held = ()
    for step in range(TICKS):
        first, last = step == 0, step == TICKS - 1
        room = spare if last else 0
        if first:
            blocks, others = prepare(
                [stream_a[0], stream_b[0], router, picks, me], ring.group, capacity
            )
            x, normed, slots, router, picks = others
            coefficient, mass, slots, packing = gates(
                normed, slots, router, picks, me, ring.group, capacity, spare
            )
        else:
            blocks, (x, coefficient) = repeat(
                [*moved, slots, router, picks, mass, me, packing], ring.group, capacity, spare, held
            )
        own = join(
            ring.across(blocks),
            capacity,
            [in_vmem(value) for value in held],
        )
        batch = [own] + [ring.within(own, h) for h in range(1, ring.group)]
        values = expert_rows(batch, up, down, capacity, experts, room, me, ring.pipe)
        held = () if last else (up, down)
        back = add_up(
            [values[0]] + [ring.within(values[h], -h) for h in range(1, ring.group)],
            experts,
            capacity,
            held,
        )
        tables = ring.over_sections(values[-1]) if last else ()
        result = finish(
            x,
            me,
            coefficient,
            ring.across(back),
            capacity,
            ring.pipe,
            tables,
            float(tokens_total) if last else 0.0,
            held,
        )
        if not last:
            moved = [ring.far(result[0]), ring.near(result[1])]
    return (result[0][None], result[1][None], result[2])


def solution(mesh):
    return jax.shard_map(
        shards,
        mesh=mesh,
        in_specs=(
            P("pipe", "expert", None),
            P("pipe", "expert", None),
            P(None, None, "pipe", "expert", None),
            P(None, "pipe", None, "expert"),
            P(None, "pipe", "expert", None),
            P(None, "pipe", None, None),
        ),
        out_specs=(P("pipe", "expert", None), P("pipe", "expert", None), P()),
        check_vma=False,
    )
```

```python
import functools

import jax
import jax.numpy as jnp
from jax import lax
from jax.experimental import pallas as pl
from jax.experimental.pallas import tpu as pltpu
from jax.sharding import PartitionSpec as P

TICKS = 2


EPS = 1e-06

LANES = 128

STREAMS = 2

EARLY_FLOPS = 2 * 10**10

TABLE_ROWS = 64


def in_hbm(array):
    return pltpu.with_memory_space_constraint(array, pltpu.HBM)


def in_vmem(array):
    return pltpu.with_memory_space_constraint(array, pltpu.VMEM)


def call(
    body, outs, name, flops=0, size=0, in_specs=None, out_specs=None, scratch=(), inputs=0, held=()
):
    more = {}
    if held:
        in_specs = [pl.BlockSpec(memory_space=pltpu.VMEM)] * (inputs + len(held))

        def whole_body(*refs):
            body(*refs[:inputs], *refs[inputs + len(held) :])

        result = call(whole_body, outs, name, flops, size, in_specs, out_specs, scratch)
        return lambda *operands: result(*operands, *[in_vmem(value) for value in held])
    if in_specs is not None:
        more["in_specs"] = in_specs
    if out_specs is not None:
        more["out_specs"] = out_specs
    return pl.pallas_call(
        body,
        out_shape=outs,
        name=name,
        scratch_shapes=scratch,
        cost_estimate=pl.CostEstimate(flops=flops, bytes_accessed=size, transcendentals=0),
        compiler_params=pltpu.CompilerParams(vmem_limit_bytes=8 << 20),
        **more,
    )


def lane_ids(rows, width=LANES):
    return lax.broadcasted_iota(jnp.int32, (rows, width), 1)


def is_even(place, shape):
    return (lax.broadcasted_iota(jnp.int32, shape, 0) * 0 + place) % 2 == 0


def upright(row):
    n = row.shape[1]
    square = jnp.broadcast_to(row, (n, n))
    diagonal = lax.broadcasted_iota(jnp.int32, (n, n), 0) == lax.broadcasted_iota(
        jnp.int32, (n, n), 1
    )
    return jnp.sum(jnp.where(diagonal, square, 0.0), axis=1, keepdims=True)


def normalize(x):
    wide = x.astype(jnp.float32)
    return (wide * lax.rsqrt(jnp.mean(wide * wide, axis=-1, keepdims=True) + EPS)).astype(
        jnp.bfloat16
    )


def chosen_by(picks):
    return [upright(picks[i : i + 1, :].astype(jnp.float32)).astype(jnp.int32) for i in range(2)]


def place_rows(chosen, mine, rows, capacity):
    lanes = lane_ids(rows)
    rows_at = lax.broadcasted_iota(jnp.int32, (rows, LANES), 0)
    kind = lanes // capacity
    named = ((chosen[0] ^ mine) == kind) | ((chosen[1] ^ mine) == kind)
    named_f = jnp.where(named, 1.0, 0.0)
    before = jnp.zeros((rows, LANES), jnp.float32)
    for r in range(rows - 1):
        before = before + jnp.where(rows_at > r, named_f[r : r + 1, :], 0.0)
    slot = named & (before == (lanes % capacity).astype(jnp.float32))
    return jnp.where(slot, 1.0, 0.0)


def turned(place, slots):
    return place.T[:slots].astype(jnp.bfloat16)


def pack_rows(turned_place, normed):
    return jnp.dot(turned_place, normed, preferred_element_type=jnp.float32)


def gate_rows(normed, router, chosen, place, me, mine, experts, capacity, spare):
    rows = normed.shape[0]
    wide = normed.astype(jnp.float32)
    taken = [jnp.zeros((rows, 1), jnp.float32) for _ in range(2)]
    for e in range(experts):
        affinity = jax.nn.sigmoid(
            jnp.sum(wide * router[e : e + 1, :].astype(jnp.float32), axis=1, keepdims=True)
        )
        taken = [jnp.where(pick == e, affinity, old) for pick, old in zip(chosen, taken)]
    whole = taken[0] + taken[1]
    shares = [taken[0] / whole, taken[1] / whole]
    kind = lane_ids(rows) // capacity
    share_at = jnp.where((chosen[0] ^ mine) == kind, shares[0], 0.0) + jnp.where(
        (chosen[1] ^ mine) == kind, shares[1], 0.0
    )
    spread = lane_ids(rows, spare)
    masses = []
    for shift in (0, experts):
        base = me * 2 * experts + shift
        here = jnp.where(spread == chosen[0] + base, shares[0], 0.0)
        here = here + jnp.where(spread == chosen[1] + base, shares[1], 0.0)
        masses.append(jnp.sum(here, axis=0, keepdims=True))
    return place * share_at, jnp.concatenate(masses)


def carry_masses(masses):
    top = masses.astype(jnp.bfloat16).astype(jnp.float32)
    return top[:1] + (masses - top)[1:]


def store_blocks(packed, block_refs, capacity):
    features = packed[0].shape[1]
    for k, block_ref in enumerate(block_refs):
        rows = [part[k * capacity : (k + 1) * capacity] for part in packed]
        block_ref[:, :features] = jnp.concatenate(rows).astype(jnp.bfloat16)


def fetch_body(group, experts, capacity, *refs):
    sources, me_ref = refs[:4], refs[4]
    x_ref, place_ref, turned_ref, router_ref, routes_ref, sems = refs[5:]
    targets = [x_ref.at[0], x_ref.at[1], router_ref, routes_ref]
    copies = [
        pltpu.make_async_copy(source, target, sems.at[i])
        for i, (source, target) in enumerate(zip(sources, targets))
    ]
    for copy in copies:
        copy.start()
    mine = lax.div(me_ref[0, 0], group)
    copies[3].wait()
    for stream in range(STREAMS):
        place = place_rows(
            chosen_by(routes_ref[0, stream]), mine, x_ref.shape[1], capacity
        )
        place_ref[stream] = place
        turned_ref[stream] = turned(place, experts * capacity)
    for copy in copies[:3]:
        copy.wait()


def fetch(inputs, group, capacity):
    x, _, router, routes, _ = inputs
    rows, features = x.shape
    experts = router.shape[1]
    outs = [
        jax.ShapeDtypeStruct((STREAMS, rows, features), jnp.bfloat16),
        jax.ShapeDtypeStruct((STREAMS, rows, LANES), jnp.float32),
        jax.ShapeDtypeStruct((STREAMS, experts * capacity, rows), jnp.bfloat16),
        jax.ShapeDtypeStruct(router.shape, router.dtype),
        jax.ShapeDtypeStruct(routes.shape, routes.dtype),
    ]
    return call(
        functools.partial(fetch_body, group, experts, capacity),
        outs,
        "fetch",
        0,
        4 * rows * features,
        [pl.BlockSpec(memory_space=pl.ANY)] * 4 + [pl.BlockSpec(memory_space=pltpu.VMEM)],
        None,
        [pltpu.SemaphoreType.DMA((4,))],
    )(*[in_hbm(value) for value in inputs[:4]], inputs[4])


def prepare_body(experts, capacity, x_ref, turned_ref, *refs):
    block_refs, normed_ref = refs[:experts], refs[experts]
    packed = []
    for stream in range(STREAMS):
        normed = normalize(x_ref[stream])
        normed_ref[stream] = normed
        packed.append(pack_rows(turned_ref[stream], normed))
    store_blocks(packed, block_refs, capacity)


def prepare(x, packing, experts, capacity):
    features = x.shape[2]
    outs = [
        jax.ShapeDtypeStruct((STREAMS * capacity, features), jnp.bfloat16) for _ in range(experts)
    ]
    outs.append(jax.ShapeDtypeStruct(x.shape, x.dtype))
    result = call(
        functools.partial(prepare_body, experts, capacity),
        outs,
        "prepare",
        EARLY_FLOPS,
        4 * x.size,
    )(x, packing)
    return result[:experts], result[experts]


def gates_body(group, experts, capacity, spare, *refs):
    normed_ref, place_ref, router_ref, routes_ref, me_ref = refs[:5]
    coefficient_ref, mass_ref, next_ref, turned_ref = refs[5:]
    me = me_ref[0, 0]
    mine = lax.div(me, group)
    rows = normed_ref.shape[1]
    for stream in range(STREAMS):
        coefficient_ref[stream], mass_ref[stream] = gate_rows(
            normed_ref[stream],
            router_ref[stream],
            chosen_by(routes_ref[0, stream]),
            place_ref[stream],
            me,
            mine,
            experts,
            capacity,
            spare,
        )
        place = place_rows(chosen_by(routes_ref[1, stream]), mine, rows, capacity)
        next_ref[stream] = place
        turned_ref[stream] = turned(place, experts * capacity)


def gates(normed, place, router, routes, me, group, capacity, spare):
    experts = router.shape[1]
    outs = [
        jax.ShapeDtypeStruct(place.shape, jnp.float32),
        jax.ShapeDtypeStruct((STREAMS, 2, spare), jnp.float32),
        jax.ShapeDtypeStruct(place.shape, jnp.float32),
        jax.ShapeDtypeStruct((STREAMS, experts * capacity, place.shape[1]), jnp.bfloat16),
    ]
    return call(
        functools.partial(gates_body, group, experts, capacity, spare),
        outs,
        "gates",
        32 * normed.size,
        4 * normed.size,
    )(normed, place, router, routes, me)


def repeat_body(group, experts, capacity, spare, *refs):
    far_ref, near_ref, place_ref, router_ref, routes_ref, old_ref, me_ref, turned_ref = refs[:8]
    block_refs = refs[8 : 8 + experts]
    x_ref, coefficient_ref = refs[8 + experts :]
    me = me_ref[0, 0]
    mine = lax.div(me, group)
    far, near = far_ref[...], near_ref[...]
    features = near.shape[1]
    even = is_even(me_ref[0, 1], near.shape)
    xs = [jnp.where(even, far, near), jnp.where(even, near, far)]
    packed, carried = [], []
    for stream in range(STREAMS):
        x_ref[stream] = xs[stream]
        normed = normalize(xs[stream])
        packed.append(pack_rows(turned_ref[stream], normed))
        coefficient, masses = gate_rows(
            normed,
            router_ref[stream],
            chosen_by(routes_ref[1, stream]),
            place_ref[stream],
            me,
            mine,
            experts,
            capacity,
            spare,
        )
        coefficient_ref[stream] = coefficient
        carried.append(
            jnp.broadcast_to(carry_masses(masses + old_ref[stream]), (capacity, spare))
        )
    store_blocks(packed, block_refs, capacity)
    carried = jnp.concatenate(carried).astype(jnp.bfloat16)
    for block_ref in block_refs:
        block_ref[:, features:] = carried


def repeat(inputs, group, capacity, spare, held):
    near, place, router = inputs[1:4]
    rows, features = near.shape
    experts = router.shape[1]
    outs = [
        jax.ShapeDtypeStruct((STREAMS * capacity, features + spare), jnp.bfloat16)
        for _ in range(experts)
    ]
    outs += [
        jax.ShapeDtypeStruct((STREAMS, rows, features), jnp.bfloat16),
        jax.ShapeDtypeStruct(place.shape, jnp.float32),
    ]
    result = call(
        functools.partial(repeat_body, group, experts, capacity, spare),
        outs,
        "prepare",
        512 * rows * features,
        4 * rows * features,
        inputs=len(inputs),
        held=held,
    )(*inputs)
    return result[:experts], result[experts:]


def order_of(experts, out):
    return [0, *range(2, experts), 1] if out else [0, *range(experts - 1, 0, -1)]


def shuffled(parts, out):
    return [parts[k] for k in order_of(len(parts), out)]


def arranged(parts, out):
    order = order_of(len(parts), out)
    return [parts[order.index(k)] for k in range(len(parts))]


def join_body(capacity, experts, *refs):
    parts, out_ref = arranged(refs[:experts], True), refs[-1]
    rows = [part[...].astype(jnp.float32) for part in parts]
    out_ref[...] = jnp.concatenate(
        [
            part[stream * capacity : (stream + 1) * capacity]
            for stream in range(STREAMS)
            for part in rows
        ]
    ).astype(out_ref.dtype)


def join(parts, capacity, after=()):
    shape = (sum(part.shape[0] for part in parts), parts[0].shape[1])
    return call(
        functools.partial(join_body, capacity, len(parts)),
        jax.ShapeDtypeStruct(shape, parts[0].dtype),
        "join",
        0,
        4 * shape[0] * shape[1],
        [pl.BlockSpec(memory_space=pltpu.VMEM)] * (len(parts) + len(after)),
    )(*shuffled(parts, True), *after)


def expert_body(group, capacity, experts, spare, layers, up_ref, down_ref, *refs):
    refs = list(refs)
    if spare:
        place_ref = refs.pop(0)
    batch_refs = refs[:group]
    out_refs = refs[group : 2 * group]
    features, hidden_width = up_ref.shape[1:]
    block = batch_refs[0].shape[0] // STREAMS
    hidden = []
    for stream in range(STREAMS):
        mine = slice(stream * block, (stream + 1) * block)
        rows = jnp.concatenate([ref[mine, :features] for ref in batch_refs])
        raw = jnp.dot(rows, up_ref[stream], preferred_element_type=jnp.float32)
        hidden.append(jax.nn.silu(raw).astype(jnp.bfloat16))
    for stream in range(STREAMS):
        mine = slice(stream * block, (stream + 1) * block)
        value = jnp.dot(hidden[stream], down_ref[stream], preferred_element_type=jnp.float32)
        for h in range(group):
            out_refs[h][mine, :] = value[h * block : (h + 1) * block].astype(jnp.bfloat16)
    if spare:
        table_ref = refs[2 * group]
        place = place_ref[0, 1]
        rows = table_ref.shape[0]
        at = lane_ids(1, spare) % experts
        lanes = lane_ids(rows)
        ladder = lax.broadcasted_iota(jnp.int32, (rows, LANES), 0)
        table = jnp.zeros((rows, LANES), jnp.float32)
        for stream in range(STREAMS):
            total = jnp.zeros((1, spare), jnp.float32)
            for ref in batch_refs:
                values = ref[:, features:].astype(jnp.float32)
                for k in range(experts):
                    row = stream * block + k * capacity
                    total = total + values[row : row + 1]
            row = place if stream == 0 else layers - 1 - place
            for e in range(experts):
                value = jnp.sum(jnp.where(at == e, total, 0.0), axis=1, keepdims=True)
                table = table + jnp.where((ladder == row) & (lanes == e), value, 0.0)
        table_ref[...] = table


def expert_rows(batch, up, down, capacity, experts, spare, place=None, layers=0):
    group = len(batch)
    features, hidden_width = up.shape[1:]
    rows = batch[0].shape[0]
    outs = [jax.ShapeDtypeStruct((rows, features), jnp.bfloat16) for _ in range(group)]
    inputs = [in_vmem(up), in_vmem(down)]
    if spare:
        outs.append(jax.ShapeDtypeStruct((-(-layers // TABLE_ROWS) * TABLE_ROWS, LANES), jnp.float32))
        inputs.append(place)
    inputs += batch
    in_place = pl.BlockSpec(memory_space=pltpu.VMEM)
    return call(
        functools.partial(expert_body, group, capacity, experts, spare, layers),
        outs,
        "experts",
        4 * group * rows * features * hidden_width,
        2 * up.size,
        [in_place] * len(inputs),
    )(*inputs)


def add_body(experts, capacity, *refs):
    parts = refs[:-experts]
    summed = sum(part[...].astype(jnp.float32) for part in parts)
    block = summed.shape[0] // STREAMS
    for k in range(experts):
        refs[len(parts) + k][...] = jnp.concatenate(
            [
                summed[stream * block + k * capacity : stream * block + (k + 1) * capacity]
                for stream in range(STREAMS)
            ]
        ).astype(jnp.bfloat16)


def add_up(parts, experts, capacity, held=()):
    rows, features = parts[0].shape
    outs = [
        jax.ShapeDtypeStruct((rows // experts, features), jnp.bfloat16) for _ in range(experts)
    ]
    return call(
        functools.partial(add_body, experts, capacity),
        outs,
        "add_up",
        0,
        4 * rows * features,
        inputs=len(parts),
        held=held,
    )(*parts)


def finish_body(experts, capacity, scale, x_ref, me_ref, coefficient_ref, *refs):
    parts = [ref[...].astype(jnp.float32) for ref in arranged(refs[:experts], False)]
    rest = refs[experts:]
    results = []
    for stream in range(STREAMS):
        returned = jnp.concatenate(
            [part[stream * capacity : (stream + 1) * capacity] for part in parts]
        ).astype(jnp.bfloat16)
        coefficient = coefficient_ref[stream, :, : experts * capacity]
        high = coefficient.astype(jnp.bfloat16).astype(jnp.float32)
        halves = jnp.concatenate([high, coefficient - high]).astype(jnp.bfloat16)
        mixtures = jnp.dot(halves, returned, preferred_element_type=jnp.float32)
        rows = high.shape[0]
        mixture = mixtures[:rows] + mixtures[rows:]
        results.append(x_ref[stream].astype(jnp.float32) + mixture)
    if not scale:
        even = is_even(me_ref[0, 1], mixture.shape)
        results = [
            jnp.where(even, results[1], results[0]),
            jnp.where(even, results[0], results[1]),
        ]
    for out_ref, result in zip(rest[-STREAMS - 1 :] if scale else rest, results):
        out_ref[...] = result.astype(out_ref.dtype)
    if scale:
        layers = rest[-1].shape[0]
        table = sum(ref[:layers, :] for ref in rest[: -STREAMS - 1])
        rest[-1][...] = table[:, :experts] / scale


def finish(x, me, coefficient, parts, capacity, layers, tables=(), scale=0.0, held=()):
    experts = len(parts)
    rows, features = coefficient.shape[1], parts[0].shape[1]
    outs = [jax.ShapeDtypeStruct((rows, features), jnp.bfloat16) for _ in range(STREAMS)]
    if scale:
        outs.append(jax.ShapeDtypeStruct((layers, experts), jnp.float32))
    return call(
        functools.partial(finish_body, experts, capacity, scale),
        outs,
        "finish",
        128 * rows * features,
        12 * rows * features,
        inputs=3 + experts + len(tables),
        held=held,
    )(x, me, coefficient, *shuffled(parts, False), *tables)


class Ring:
    def __init__(self, experts):
        self.pipe = lax.axis_size("pipe")
        self.size = lax.axis_size("expert")
        self.experts = experts
        self.group = self.size // experts

    def across(self, blocks):
        moved = {0: blocks[0]}
        for k in sorted(range(1, self.experts), key=lambda k: -k):
            moved[k] = lax.ppermute(
                blocks[k], "expert", [(j, j ^ (k * self.group)) for j in range(self.size)]
            )
        return [moved[k] for k in range(self.experts)]

    def within(self, array, shift):
        pairs = [
            (j, j // self.group * self.group + (j + shift) % self.group) for j in range(self.size)
        ]
        return lax.ppermute(array, "expert", pairs)

    def far(self, array):
        steps = [(i + 1 if i % 2 else i - 1) % self.pipe for i in range(self.pipe)]
        return lax.ppermute(array, "pipe", list(enumerate(steps)))

    def near(self, array):
        return lax.ppermute(array, "pipe", [(i, i ^ 1) for i in range(self.pipe)])

    def over_sections(self, table):
        if self.pipe & (self.pipe - 1):
            return [lax.psum(table, "pipe")]
        parts = [table]
        step = 1
        while step < self.pipe:
            table = sum(parts[1:], parts[0])[: table.shape[0] if step == 1 else self.pipe]
            moved = lax.ppermute(table, "pipe", [(i, i ^ step) for i in range(self.pipe)])
            parts = [table, moved]
            step *= 2
        return parts


def shards(stream_a, stream_b, routes, up_weight, down_weight, router_weight):
    experts = router_weight.shape[-1]
    ring = Ring(experts)
    rows, features = stream_a.shape[1:]
    capacity = rows * routes.shape[-1] // experts
    me = jnp.stack([lax.axis_index("expert"), lax.axis_index("pipe")]).astype(jnp.int32)[None]
    router = jnp.swapaxes(router_weight[:, 0], 1, 2)
    picks = jnp.swapaxes(routes[:, :, 0], 2, 3)
    spare = -(-2 * experts * ring.size // LANES) * LANES
    tokens_total = 2 * TICKS * rows * ring.size
    up, down = up_weight[:, 0], down_weight[:, 0]
    held = ()
    for step in range(TICKS):
        first, last = step == 0, step == TICKS - 1
        room = spare if last else 0
        if first:
            x, slots, packing, router, picks = fetch(
                [stream_a[0], stream_b[0], router, picks, me], ring.group, capacity
            )
            blocks, normed = prepare(x, packing, experts, capacity)
            coefficient, mass, slots, packing = gates(
                normed, slots, router, picks, me, ring.group, capacity, spare
            )
        else:
            blocks, (x, coefficient) = repeat(
                [*moved, slots, router, picks, mass, me, packing], ring.group, capacity, spare, held
            )
        own = join(
            ring.across(blocks),
            capacity,
            [in_vmem(value) for value in held],
        )
        batch = [own] + [ring.within(own, h) for h in range(1, ring.group)]
        values = expert_rows(batch, up, down, capacity, experts, room, me, ring.pipe)
        held = () if last else (up, down)
        back = add_up(
            [values[0]] + [ring.within(values[h], -h) for h in range(1, ring.group)],
            experts,
            capacity,
            held,
        )
        tables = ring.over_sections(values[-1]) if last else ()
        result = finish(
            x,
            me,
            coefficient,
            ring.across(back),
            capacity,
            ring.pipe,
            tables,
            float(tokens_total) if last else 0.0,
            held,
        )
        if not last:
            moved = [ring.far(result[0]), ring.near(result[1])]
    return (result[0][None], result[1][None], result[2])


def solution(mesh):
    return jax.shard_map(
        shards,
        mesh=mesh,
        in_specs=(
            P("pipe", "expert", None),
            P("pipe", "expert", None),
            P(None, None, "pipe", "expert", None),
            P(None, "pipe", None, "expert"),
            P(None, "pipe", "expert", None),
            P(None, "pipe", None, None),
        ),
        out_specs=(P("pipe", "expert", None), P("pipe", "expert", None), P()),
        check_vma=False,
    )
```
